256 devices in a mesh: lat: 16 (over z, y_hi), lon: 16 (over y_lo, x, core).
Axes of the slice: x: 4, y: 4 (y_hi: 2, y_lo: 2; y = y_hi * 2 + y_lo), z: 8, core: 2. Of those that a mesh axis runs over, the one named last changes fastest.
Arguments:
- fields: bfloat16 [2, 4, 192, 192, 512], P(None, None, 'lat', 'lon'), may hold values from -6 to 6
- valid_rows: int32 [192], P('lat'), may hold values from 0 to 1, as said below
- fine_qkv: bfloat16 [512, 1536], replicated, may hold values from -1 to 1
- fine_out: bfloat16 [512, 512], replicated, may hold values from -0.25 to 0.25
- merge_weight: bfloat16 [2048, 1024], replicated, may hold values from -0.125 to 0.125
- coarse_qkv: bfloat16 [3, 1024, 1024], P(None, 'lat', 'lon'), may hold values from -1 to 1
- coarse_out: bfloat16 [1024, 1024], P('lat', 'lon'), may hold values from -0.1875 to 0.1875
- expand_weight: bfloat16 [1024, 2048], replicated, may hold values from -0.1875 to 0.1875
Outputs:
- decoded: bfloat16 [2, 4, 192, 192, 512], P(None, None, 'lat', 'lon')
The draws below stay inside these ranges and needn't reach their ends.
Inputs may be any that keep to these rules, and one draw needn't show every extreme that they name: `valid_rows`: the rows with value 1 are the first ones; between 1 and 18 rows at the end are 0.
All inputs are finite; a program needn't handle non-finite values.
Results may differ from the reference program's by a relative error of at most 0.01.
Values may be sent and summed in bfloat16 or wider, within the bound.
A program may use at most 128 MiB of HBM per device.

```python
import math
import jax
import jax.numpy as jnp
from jax import lax

D = 512
D2 = 1024
HEAD_DIM = 32
LEV = 4
WIN_LEV = 2
WIN_LAT = 6
WIN_LON = 12
LAT_DEV = 12
SAMPLES = 2
NLAT = 192
NLON = 192


def draw_valid_rows(key, part):
    key = jax.random.fold_in(key, 3)
    count = jax.random.randint(key, (), NLAT - 3 * LAT_DEV // 2, NLAT)
    return (jnp.arange(NLAT) < count).astype(jnp.int32)


def draw_fine_qkv(key, part):
    key = jax.random.fold_in(key, 5)
    first = jax.random.fold_in(key, 0)
    drawn = jax.random.normal(first, (D, 3 * D), jnp.float32)
    return jnp.clip(drawn / math.sqrt(D), -1.0, 1.0).astype(jnp.bfloat16)


def draw_coarse_qkv(key, part):
    key = jax.random.fold_in(key, 7)
    first = jax.random.fold_in(key, 0)
    drawn = jax.random.normal(first, (D2, 3 * D2), jnp.float32)
    scaled = jnp.clip(drawn / math.sqrt(D2), -1.0, 1.0)
    return scaled.reshape(D2, 3, D2).transpose(1, 0, 2).astype(jnp.bfloat16)


def level_of(rng, dims, pieces, smallest, largest):
    def one(dim, shards_of):
        draws = jax.random.uniform(jax.random.fold_in(jax.random.fold_in(rng, 6), dim), (shards_of,), jnp.float32, smallest / len(pieces), largest / len(pieces))
        return jnp.repeat(jnp.exp(draws), dims[dim] // shards_of).reshape((-1,) + (1,) * (len(dims) - dim - 1))

    level = one(*pieces[0])
    for cut in pieces[1:]:
        level = level * one(*cut)
    return level


def noise(stream_key, extent, scale, limit, pieces=(), kind=jnp.bfloat16):
    level = level_of(stream_key, extent, pieces, -0.22, 0.18) if pieces else 1.0
    entries = jax.random.normal(stream_key, extent, jnp.float32) * scale * level
    return jnp.minimum(jnp.maximum(entries, -limit), limit).astype(kind)


def setup_inputs(seed: int = 0) -> dict:
    keys = jax.random.split(jax.random.key(seed), 9)
    fields = noise(keys[0], (SAMPLES, LEV, NLAT, NLON, D), 1.0, 6.0, ((2, 16), (3, 16)))
    valid_rows = draw_valid_rows(jax.random.fold_in(keys[8], 71), 0)
    fine_qkv = draw_fine_qkv(jax.random.fold_in(keys[8], 71), 0)
    fine_out = noise(keys[3], (D, D), D ** -0.5, 0.25)
    merge_weight = noise(keys[4], (4 * D, D2), (4 * D) ** -0.5, 0.125)
    coarse_qkv = draw_coarse_qkv(jax.random.fold_in(keys[8], 71), 0)
    coarse_out = noise(keys[6], (D2, D2), D2 ** -0.5, 0.1875, ((0, 16), (1, 16)))
    expand_weight = noise(keys[7], (D2, 4 * D), D2 ** -0.5, 0.1875)
    return dict(fields=fields, valid_rows=valid_rows, fine_qkv=fine_qkv, fine_out=fine_out, merge_weight=merge_weight, coarse_qkv=coarse_qkv, coarse_out=coarse_out, expand_weight=expand_weight)


def layer_norm(values):
    values = values.astype(jnp.float32)
    centre = values - lax.optimization_barrier(jnp.mean(values, axis=-1, keepdims=True))
    spread = lax.optimization_barrier(jnp.mean(centre * centre, axis=-1, keepdims=True))
    return centre * lax.rsqrt(spread + 1e-05)

def attend(queries, keys_all, values, allowed, scale):
    scores = jnp.einsum('bqhd,bkhd->bhqk', queries.astype(jnp.float32), keys_all.astype(jnp.float32)) * scale
    scores = jnp.where(allowed[:, None], scores, -jnp.inf)
    highest = lax.optimization_barrier(jnp.max(scores, axis=-1, keepdims=True))
    expo = jnp.exp(scores - highest)
    weights = (expo / lax.optimization_barrier(jnp.sum(expo, axis=-1, keepdims=True))).astype(jnp.bfloat16)
    mixed = jnp.einsum('bhqk,bkhd->bqhd', weights.astype(jnp.float32), values.astype(jnp.float32)).astype(jnp.bfloat16)
    return mixed.reshape(mixed.shape[0], mixed.shape[1], -1)

def reference(fields, valid_rows, fine_qkv, fine_out, merge_weight, coarse_qkv, coarse_out, expand_weight):
    half_lev = WIN_LEV // 2
    half_lat = WIN_LAT // 2
    half_lon = WIN_LON // 2
    heads = D // HEAD_DIM
    heads_two = D2 // HEAD_DIM
    scale = HEAD_DIM ** (-0.5)
    lev_groups = LEV // WIN_LEV
    lat_windows = NLAT // WIN_LAT
    lon_windows = NLON // WIN_LON
    shape_three = (WIN_LEV, WIN_LAT, WIN_LON)
    qkv_flat = coarse_qkv.transpose(1, 0, 2).reshape(D2, 3 * D2)
    shifted = jnp.roll(fields, (-half_lev, -half_lat, -half_lon), axis=(1, 2, 3))
    blocks = shifted.reshape(SAMPLES, lev_groups, WIN_LEV, lat_windows, WIN_LAT, NLON, D)
    blocks = blocks.transpose(0, 1, 3, 2, 4, 5, 6).reshape(-1, WIN_LEV, WIN_LAT, NLON, D)
    level_ids = ((jnp.arange(LEV) + half_lev) % LEV + half_lev) // WIN_LEV
    row_global = (jnp.arange(NLAT) + half_lat) % NLAT
    row_ids = (row_global + half_lat) // WIN_LAT
    row_valid = valid_rows[row_global]
    grid = (SAMPLES, lev_groups, lat_windows)
    block_levels = jnp.broadcast_to(level_ids.reshape(1, lev_groups, 1, WIN_LEV), grid + (WIN_LEV,)).reshape(-1, WIN_LEV)
    block_rows = jnp.broadcast_to(row_ids.reshape(1, 1, lat_windows, WIN_LAT), grid + (WIN_LAT,)).reshape(-1, WIN_LAT)
    block_valid = jnp.broadcast_to(row_valid.reshape(1, 1, lat_windows, WIN_LAT), grid + (WIN_LAT,)).reshape(-1, WIN_LAT)

    def fine_block(inputs):
        tokens, lev_id, row_id, row_ok = inputs
        windows = tokens.reshape(WIN_LEV, WIN_LAT, lon_windows, WIN_LON, D).transpose(2, 0, 1, 3, 4).reshape(lon_windows, -1, D)
        token_level = jnp.broadcast_to(lev_id[:, None, None], shape_three).reshape(-1)
        token_row = jnp.broadcast_to(row_id[None, :, None], shape_three).reshape(-1)
        token_valid = jnp.broadcast_to(row_ok[None, :, None], shape_three).reshape(-1)
        allowed = (token_level[:, None] == token_level[None, :]) & (token_row[:, None] == token_row[None, :])
        allowed = allowed & ((token_valid[None, :] == 1) | (token_valid[:, None] == 0))
        allowed = jnp.broadcast_to(allowed, (lon_windows,) + allowed.shape)
        normed = layer_norm(windows).astype(jnp.bfloat16)
        projected = jnp.dot(normed.reshape(-1, D), fine_qkv, preferred_element_type=jnp.float32)
        projected = projected.astype(jnp.bfloat16).reshape(lon_windows, -1, 3, heads, HEAD_DIM)
        mixed = attend(projected[:, :, 0], projected[:, :, 1], projected[:, :, 2], allowed, scale)
        update = jnp.dot(mixed.reshape(-1, D), fine_out, preferred_element_type=jnp.float32).reshape(windows.shape)
        keep = token_valid.astype(jnp.float32)[None, :, None]
        result = ((windows.astype(jnp.float32) + update) * keep).astype(jnp.bfloat16)
        result = result.reshape(lon_windows, WIN_LEV, WIN_LAT, WIN_LON, D).transpose(1, 2, 0, 3, 4)
        return result.reshape(WIN_LEV, WIN_LAT, NLON, D)
    skipped = lax.map(fine_block, (blocks, block_levels, block_rows, block_valid))
    skipped = skipped.reshape(SAMPLES, lev_groups, lat_windows, WIN_LEV, WIN_LAT, NLON, D)
    skipped = skipped.transpose(0, 1, 3, 2, 4, 5, 6).reshape(SAMPLES, LEV, NLAT, NLON, D)
    skip = jnp.roll(skipped, (half_lev, half_lat, half_lon), axis=(1, 2, 3))
    band_rows = 2 * WIN_LAT
    bands = NLAT // band_rows
    coarse_cols = NLON // 2
    coarse_windows = coarse_cols // WIN_LON
    coarse_blocks = skip.reshape(SAMPLES, lev_groups, WIN_LEV, bands, band_rows, NLON, D)
    coarse_blocks = coarse_blocks.transpose(0, 1, 3, 2, 4, 5, 6).reshape(-1, WIN_LEV, band_rows, NLON, D)
    band_valid = jnp.broadcast_to(valid_rows.reshape(1, 1, bands, band_rows), (SAMPLES, lev_groups, bands, band_rows)).reshape(-1, band_rows)

    def coarse_block(inputs):
        tokens, row_ok = inputs
        parts = tokens.reshape(WIN_LEV, WIN_LAT, 2, coarse_cols, 2, D).transpose(0, 1, 3, 4, 2, 5).reshape(-1, 4 * D)
        merged = jnp.dot(layer_norm(parts).astype(jnp.bfloat16), merge_weight, preferred_element_type=jnp.float32).astype(jnp.bfloat16)
        windows = merged.reshape(WIN_LEV, WIN_LAT, coarse_windows, WIN_LON, D2).transpose(2, 0, 1, 3, 4).reshape(coarse_windows, -1, D2)
        coarse_ok = row_ok[0::2]
        token_valid = jnp.broadcast_to(coarse_ok[None, :, None], shape_three).reshape(-1)
        allowed = (token_valid[None, :] == 1) | (token_valid[:, None] == 0)
        allowed = jnp.broadcast_to(allowed, (coarse_windows,) + allowed.shape)
        normed = layer_norm(windows).astype(jnp.bfloat16)
        projected = jnp.dot(normed.reshape(-1, D2), qkv_flat, preferred_element_type=jnp.float32)
        projected = projected.astype(jnp.bfloat16).reshape(coarse_windows, -1, 3, heads_two, HEAD_DIM)
        mixed = attend(projected[:, :, 0], projected[:, :, 1], projected[:, :, 2], allowed, scale)
        update = jnp.dot(mixed.reshape(-1, D2), coarse_out, preferred_element_type=jnp.float32).reshape(windows.shape)
        coarse = (windows.astype(jnp.float32) + update).astype(jnp.bfloat16)
        grown = jnp.dot(coarse.reshape(-1, D2), expand_weight, preferred_element_type=jnp.float32)
        grown = grown.reshape(coarse_windows, WIN_LEV, WIN_LAT, WIN_LON, 2, 2, D).transpose(1, 2, 0, 3, 4, 5, 6)
        grown = grown.reshape(WIN_LEV, WIN_LAT, coarse_cols, 2, 2, D).transpose(0, 1, 4, 2, 3, 5).reshape(WIN_LEV, band_rows, NLON, D)
        keep = row_ok.astype(jnp.float32)[None, :, None, None]
        return ((tokens.astype(jnp.float32) + grown) * keep).astype(jnp.bfloat16)
    decoded = lax.map(coarse_block, (coarse_blocks, band_valid))
    decoded = decoded.reshape(SAMPLES, lev_groups, bands, WIN_LEV, band_rows, NLON, D)
    return decoded.transpose(0, 1, 3, 2, 4, 5, 6).reshape(SAMPLES, LEV, NLAT, NLON, D)
```

```python
import math

import jax
import jax.numpy as jnp
import numpy as np
from jax import lax
from jax.experimental import pallas as pl
from jax.experimental.pallas import tpu as pltpu
from jax.sharding import PartitionSpec as P

BF = jnp.bfloat16
F32 = jnp.float32
MESH = pl.DeviceIdType.MESH
EPSILON = 1e-05
NEG = -1e30
QSCALE = 32 ** (-0.5) * math.log2(math.e)

SEG = (0, 112, 224, 272, 320)
LEVELS = ((1, 2), (3, 0))
PADC = 80


def segment_row(l2, r, c):
    if r >= 3:
        base, rows, row = (0, 9, r - 3) if c >= 6 else (112, 9, r - 3)
    else:
        base, rows, row = (224, 3, r) if c >= 6 else (272, 3, r)
    return base + (l2 * rows + row) * 6 + c % 6


def window_row(l2, r, c):
    window, row = (0, r - 3) if 3 <= r < 9 else (1, r - 9 if r >= 9 else r + 3)
    column = c - 6 if c >= 6 else c + 6
    return window * 144 + l2 * 72 + row * 12 + column


def coarse_row(level, row, column):
    return (level // 2) * PADC + (level % 2) * 36 + row * 6 + column


def tables():
    p1 = np.zeros((2, 320, 192), np.float32)
    p2 = np.zeros((288, 320), np.float32)
    p4 = np.zeros((4 * 2 * PADC, 640), np.float32)
    p5 = np.zeros((768, 4 * 2 * PADC), np.float32)
    for r in range(12):
        for c in range(12):
            plane = (r % 2) + 2 * (c % 2)
            for l2 in range(2):
                seg = segment_row(l2, r, c)
                p1[l2, seg, r * 16 + c] = 1
                p2[window_row(l2, r, c), seg] = 1
                for lg in range(2):
                    level = LEVELS[lg][l2]
                    low = plane * 2 * PADC + coarse_row(level, r // 2, c // 2)
                    p4[low, lg * 320 + seg] = 1
                    p5[level * 192 + r * 16 + c, low] = 1
    rows = np.zeros((2, 144, 32), np.float32)
    differ = np.zeros((144, 144), np.float32)
    level = np.zeros((144, 144), np.float32)
    for t in range(144):
        r6 = (t % 72) // 12
        rows[0, t, 3 + r6] = 1
        rows[1, t, 9 + r6 if r6 < 3 else 16 + r6 - 3] = 1
        for u in range(144):
            differ[t, u] = (r6 < 3) != ((u % 72) // 12 < 3)
            level[t, u] = (t // 72) != (u // 72)
    rows_t = np.zeros((2, 256, 144), np.float32)
    rows_t[:, 0:12] = rows.transpose(0, 2, 1)[:, 0:12]
    rows_t[:, 128:131] = rows.transpose(0, 2, 1)[:, 16:19]
    coarse = np.zeros((PADC, 16), np.float32)
    keep = np.zeros((2, 2 * PADC, 16), np.float32)
    for t in range(72):
        row = (t % 36) // 6
        coarse[t, 2 * row] = 1
        for group in range(2):
            for parity in range(2):
                keep[parity, group * PADC + t, 2 * row + parity] = 1
    coarse_t = np.zeros((128, 2 * PADC), np.float32)
    coarse_t[0:16, :PADC] = coarse.T
    coarse_t[0:16, PADC:] = coarse.T
    pads = np.zeros((8, 2 * PADC), np.float32)
    pads[:, np.arange(2 * PADC) % PADC >= 72] = 1
    half = [jnp.asarray(a, BF) for a in (p1, rows, rows_t, coarse, coarse_t, keep)]
    full = [jnp.asarray(a, F32) for a in (level, differ, pads)]
    late = [jnp.asarray(a, BF) for a in (p2, p2.T.copy(), p4, p5)]
    return half + full, late


def dot(a, b):
    return jnp.dot(a, b, preferred_element_type=F32)


def dot_nt(a, b):
    return lax.dot_general(a, b, (((1,), (1,)), ((), ())), preferred_element_type=F32)


def normalised(x, width):
    mean = jnp.sum(x, axis=-1, keepdims=True) * (1.0 / width)
    centre = x - mean
    spread = jnp.sum(centre * centre, axis=-1, keepdims=True) * (1.0 / width)
    return centre * lax.rsqrt(spread + EPSILON)


def attention(q4, k4, v4, bias):
    count, keys = q4.shape[0], k4.shape[0]
    head = lax.broadcasted_iota(jnp.int32, (16, 128), 1) // 32
    stacked = []
    for h in range(4):
        mask = jnp.where(head == h, 1.0, 0.0).astype(BF)[0:1]
        stacked.append(q4 * mask)
    scores = dot_nt(jnp.concatenate(stacked, axis=0), k4).reshape(4, count, keys) + bias[None]
    highest = jnp.max(scores, axis=-1, keepdims=True)
    expo = jnp.exp2(scores - highest).astype(BF).reshape(4 * count, keys)
    values = jnp.concatenate([v4, jnp.ones((keys, 128), BF)], axis=1)
    mixed = dot(expo, values)
    lanes = lax.broadcasted_iota(jnp.int32, (count, 128), 1) // 32
    top, low = mixed[:count, :128], mixed[:count, 128:]
    for h in range(1, 4):
        part = mixed[h * count : (h + 1) * count]
        top = jnp.where(lanes == h, part[:, :128], top)
        low = jnp.where(lanes == h, part[:, 128:], low)
    return (top / low).astype(BF)


def kernel(
    xp, fl, cw, p1, r1, rt, rc, rct, rk, lm, dm, pads,
    p2_h, p3_h, p4_h, p5_h, wqkv_h, wo_h, wm_h, we_h,
    out,
    p2, p3, p4, p5, wqkv, wo, wm, we,
    snd, xb, ret, zb, fln, pb, wg,
    xw, q, k, v, at, kcol, bias, cbias, krow,
    skp, nbm, mg, n2, q2, kv2, a2, co, dc,
    hs, hr, rs, rr, fs, fr, ps, pr, zs, zr, s2s, s2r, s3s, s3r, ls, lr, ds_, dr, ns, nr, ws,
):
    lat = lax.axis_index("lat")
    lon = lax.axis_index("lon")
    z, y_hi = lat // 2, lat % 2
    y_lo, x, c = lon // 8, (lon // 2) % 4, lon % 2
    y = y_hi * 2 + y_lo

    def device(z_, y_, x_, c_):
        return (z_ * 2 + y_ // 2, (y_ % 2) * 8 + x_ * 2 + c_)

    north, south = (lat + 15) % 16, (lat + 1) % 16
    west, east = (lon + 15) % 16, (lon + 1) % 16
    partner = device(z, y, x, 1 - c)

    barrier = pltpu.get_barrier_semaphore()
    greeted = [partner, (lat, west), (lat, east), (north, lon), (south, lon), (north, west), (south, east)]
    greeted += [device((z + d) % 8, y, x, c) for d in range(1, 8)]
    greeted += [device(z, (y + d) % 4, x, c) for d in range(1, 4)]
    greeted += [device(z, y, (x + d) % 4, c) for d in range(1, 4)]
    for target in greeted:
        pl.semaphore_signal(barrier, inc=1, device_id=target, device_id_type=MESH)

    late = list(zip((p2_h, wqkv_h, wo_h, p3_h, p4_h, wm_h, we_h, p5_h), (p2, wqkv, wo, p3, p4, wm, we, p5)))
    loads = [pltpu.make_async_copy(a, b, ws.at[n]) for n, (a, b) in enumerate(late)]
    for copy in loads:
        copy.start()

    def remote(src, dst, send, recv, target):
        return pltpu.make_async_remote_copy(
            src_ref=src, dst_ref=dst, send_sem=send, recv_sem=recv, device_id=target, device_id_type=MESH
        )

    def halo(i):
        targets = ((lat, west), (north, lon), (north, west))
        return [
            remote(snd.at[i, SEG[n + 1] : SEG[n + 2]], xb.at[i, SEG[n + 1] : SEG[n + 2]], hs.at[i, n], hr.at[i, n], targets[n])
            for n in range(3)
        ]

    def back(i):
        targets = ((lat, east), (south, lon), (south, east))
        return [
            remote(ret.at[i, SEG[n + 1] : SEG[n + 2]], zb.at[i, SEG[n + 1] : SEG[n + 2]], rs.at[i, n], rr.at[i, n], targets[n])
            for n in range(3)
        ]

    flags = remote(fl, fln, fs.at[0], fr.at[0], (north, lon))
    pair = remote(cw, pb, ps.at[0], pr.at[0], partner)

    def along_z():
        block = wg.at[y_lo, x, :, z, y_hi, c]
        return [remote(block, block, zs.at[d - 1], zr.at[d - 1], device((z + d) % 8, y, x, c)) for d in range(1, 8)]

    def second():
        block = wg.at[y_lo, x, :, :, y_hi, c]
        return [
            remote(block, block, s2s.at[d - 1], s2r.at[d - 1], device(z, (y + d * (1 - c)) % 4, (x + d * c) % 4, c))
            for d in range(1, 4)
        ]

    def chunk(core, step, matrices):
        if core == 0:
            return wg.at[:, (x + step) % 4, matrices, :, :, 0]
        other = (y + step) % 4
        return wg.at[other % 2, :, matrices, :, other // 2, 1]

    def ring(core, step):
        return device(z, y, (x + step) % 4, core) if core == 0 else device(z, (y + step) % 4, x, core)

    every = slice(0, 4)

    def third(core):
        block = chunk(core, 0, every)
        return [remote(block, block, s3s.at[n], s3r.at[n], ring(core, step)) for n, step in enumerate((1, 3))]

    def relay(core):
        moves = ((1, 3, slice(0, 2)), (3, 1, slice(2, 4)))
        return [
            remote(chunk(core, s, m), chunk(core, s, m), ls.at[n], lr.at[n], ring(core, to))
            for n, (to, s, m) in enumerate(moves)
        ]

    def across(core, n):
        block = chunk(core, (0, 3, 1, 2)[n], every)
        return remote(block, block, ds_.at[n], dr.at[n], partner)

    def on_core(action):
        @pl.when(c == 0)
        def _():
            action(0)

        @pl.when(c == 1)
        def _():
            action(1)

    pl.semaphore_wait(barrier, len(greeted))
    pair.start()
    flags.start()

    for i in range(4):
        s, (first, last) = i // 2, LEVELS[i % 2]
        tokens = (dot(p1[0], xp[s, first]) + dot(p1[1], xp[s, last])).astype(BF)
        snd[i] = tokens
        xb[i, 0:112] = tokens[0:112]
        for copy in halo(i):
            copy.start()

    pair.wait_recv()
    block = cw[...] + pb[...]
    wg[y_lo, x, :, z, y_hi, c] = jnp.where(c == 0, block[:, :32], block[:, 32:])
    for copy in along_z():
        copy.start()

    flags.wait_recv()
    own, following = fl[...], fln[...]
    seam = jnp.where(lat == 15, NEG, 0.0)
    for w in range(2):
        down = dot(r1[w, :, 0:16], own[0:16]) + dot(r1[w, :, 16:32], following[0:16])
        flat = dot(own[16:32], rt[w, 0:128]) + dot(following[16:32], rt[w, 128:256])
        kcol[w * 144 : (w + 1) * 144] = down
        forbid = ((1.0 - flat[0:1]) * down[:, 0:1]) * NEG
        if w == 1:
            forbid = forbid + dm[...] * seam
        bias[0, w] = forbid
        bias[1, w] = forbid + lm[...] * NEG
    down = dot(rc[...], own[0:16])
    flat = dot(own[16:32], rct[...])
    cbias[...] = ((1.0 - flat[0:1]) * down[:, 0:1] + pads[0:1]) * NEG
    for parity in range(2):
        krow[parity] = dot(rk[parity], own[0:16])

    for copy in loads[0:4]:
        copy.wait()

    def fine(i, carry):
        @pl.when(i == 1)
        def _():
            for copy in along_z():
                copy.wait_recv()
            for copy in second():
                copy.start()

        @pl.when(i == 2)
        def _():
            for copy in second():
                copy.wait_recv()

            def go(core):
                for copy in third(core):
                    copy.start()
                across(core, 0).start()

            on_core(go)

        for copy in halo(i):
            copy.wait_recv()
        tokens = dot(p2[...], xb[i])
        xw[...] = tokens
        normed = normalised(tokens, 512).astype(BF)
        q[...] = (dot(normed, wqkv[:, 0:512]) * QSCALE).astype(BF)
        k[...] = dot(normed, wqkv[:, 512:1024]).astype(BF)
        v[...] = dot(normed, wqkv[:, 1024:1536]).astype(BF)
        group = i % 2

        def heads(g, carry):
            lanes = pl.ds(pl.multiple_of(g * 128, 128), 128)
            for w in range(2):
                rows = slice(w * 144, (w + 1) * 144)
                at[rows, lanes] = attention(q[rows, lanes], k[rows, lanes], v[rows, lanes], bias[group, w])
            return carry

        lax.fori_loop(0, 4, heads, 0)
        skip = ((xw[...] + dot(at[...], wo[...])) * kcol[:, 0:1]).astype(BF)
        tokens = dot(p3[...], skip).astype(BF)
        ret[i] = tokens
        zb[i, 0:112] = tokens[0:112]
        for copy in back(i):
            copy.start()
        return carry

    lax.fori_loop(0, 4, fine, 0)

    def go(core):
        for copy in third(core):
            copy.wait_recv()
        for copy in relay(core):
            copy.start()
        across(core, 1).start()
        across(core, 2).start()

    on_core(go)
    for copy in loads[4:]:
        copy.wait()

    for s in range(2):
        for i in (2 * s, 2 * s + 1):
            for copy in back(i):
                copy.wait_recv()
        planes = dot(p4[...], zb[2 * s : 2 * s + 2].reshape(640, 512))
        skp[s] = planes.astype(BF)
        planes = planes.reshape(4, 160, 512)
        mean = jnp.sum(jnp.sum(planes, axis=0), axis=-1, keepdims=True) * (1.0 / 2048)
        centre = planes - mean[None]
        spread = jnp.sum(jnp.sum(centre * centre, axis=0), axis=-1, keepdims=True) * (1.0 / 2048)
        nbm[:, s * 160 : (s + 1) * 160] = (centre * lax.rsqrt(spread + EPSILON)[None]).astype(BF)

    def merge(n, carry):
        lanes = pl.ds(pl.multiple_of(n * 256, 256), 256)
        total = dot(nbm[0], wm[0:512, lanes])
        for p in range(1, 4):
            total = total + dot(nbm[p], wm[512 * p : 512 * (p + 1), lanes])
        mg[:, lanes] = total.astype(BF)
        return carry

    lax.fori_loop(0, 4, merge, 0)
    n2[0] = normalised(mg[...].astype(F32), 1024).astype(BF)
    swap = remote(n2.at[0], n2.at[1], ns.at[0], nr.at[0], partner)
    swap.start()

    def go(core):
        for copy in relay(core):
            copy.wait_recv()
        across(core, 3).start()

    on_core(go)

    def go(core):
        for n in range(4):
            across(core, n).wait_recv()

    on_core(go)

    def weights(matrix, n):
        low = (n % 2) * 2
        pieces = [wg[n // 2, low + j, matrix].reshape(1024, 128) for j in range(2)]
        return jnp.concatenate(pieces, axis=1)

    def queries(n, carry):
        lanes = pl.ds(pl.multiple_of(n * 256, 256), 256)
        q2[:, lanes] = (dot(n2[0], weights(0, n)) * QSCALE).astype(BF)
        return carry

    lax.fori_loop(0, 4, queries, 0)
    swap.wait_recv()

    def keys(n, carry):
        matrix, block = n // 4, n % 4
        lanes = pl.ds(pl.multiple_of(block * 256, 256), 256)
        kv2[matrix, :, lanes] = dot(n2[...].reshape(640, 1024), weights(matrix + 1, block)).astype(BF)
        return carry

    lax.fori_loop(0, 8, keys, 0)

    def heads(g, carry):
        lanes = pl.ds(pl.multiple_of(g * 128, 128), 128)
        for j in range(4):
            rows, far = slice(j * PADC, (j + 1) * PADC), slice(320 + j * PADC, 320 + (j + 1) * PADC)
            k4 = jnp.concatenate([kv2[0, rows, lanes], kv2[0, far, lanes]], axis=0)
            v4 = jnp.concatenate([kv2[1, rows, lanes], kv2[1, far, lanes]], axis=0)
            a2[rows, lanes] = attention(q2[rows, lanes], k4, v4, cbias[...])
        return carry

    lax.fori_loop(0, 8, heads, 0)

    def project(n, carry):
        lanes = pl.ds(pl.multiple_of(n * 256, 256), 256)
        co[:, lanes] = (mg[:, lanes].astype(F32) + dot(a2[...], weights(3, n))).astype(BF)
        return carry

    lax.fori_loop(0, 4, project, 0)

    def expand(n, carry):
        plane, side = n // 2, n % 2
        grown = dot(co[...], we[:, pl.ds(pl.multiple_of(n * 256, 256), 256)])
        rows = pl.ds(pl.multiple_of(plane * 160, 160), 160)
        lanes = pl.ds(pl.multiple_of(side * 256, 256), 256)
        keep = krow[plane % 2][:, 0:1]
        for s in range(2):
            dc[s, rows, lanes] = ((skp[s, rows, lanes].astype(F32) + grown[s * 160 : (s + 1) * 160]) * keep).astype(BF)
        return carry

    lax.fori_loop(0, 8, expand, 0)
    for s in range(2):
        out[s] = dot(p5[...], dc[s]).astype(BF)

    pair.wait_send()
    flags.wait_send()
    swap.wait_send()
    for i in range(4):
        for copy in halo(i) + back(i):
            copy.wait_send()
    for copy in along_z() + second():
        copy.wait_send()

    def go(core):
        for copy in third(core) + relay(core) + [across(core, n) for n in range(4)]:
            copy.wait_send()

    on_core(go)


def shards(fields, valid_rows, fine_qkv, fine_out, merge_weight, coarse_qkv, coarse_out, expand_weight):
    early, late = tables()
    xp = jnp.pad(fields, ((0, 0), (0, 0), (0, 0), (0, 4), (0, 0))).reshape(2, 4, 192, 512)
    valid = jnp.pad(valid_rows, (0, 4)).astype(BF)
    fl = jnp.concatenate(
        [jnp.broadcast_to(valid[:, None], (16, 128)), jnp.broadcast_to(jnp.pad(valid, (0, 112))[None], (16, 128))], axis=0
    )
    block = jnp.concatenate([coarse_qkv, coarse_out[None]], axis=0)
    is_first = lax.axis_index("lon") % 2 == 0
    cw = jnp.where(
        is_first, jnp.pad(block, ((0, 0), (0, 0), (0, 64))), jnp.pad(block, ((0, 0), (0, 0), (64, 0)))
    )
    operands = [xp, fl, cw] + early + late + [fine_qkv, fine_out, merge_weight, expand_weight]
    vmem = pl.BlockSpec(memory_space=pltpu.VMEM)
    anywhere = pl.BlockSpec(memory_space=pl.ANY)
    dma = pltpu.SemaphoreType.DMA
    scratch = [pltpu.VMEM(a.shape, BF) for a in late]
    scratch += [pltpu.VMEM(a.shape, BF) for a in (fine_qkv, fine_out, merge_weight, expand_weight)]
    scratch += [pltpu.VMEM((4, 320, 512), BF)] * 4
    scratch += [pltpu.VMEM((32, 128), BF), pltpu.VMEM((4, 64, 128), BF)]
    scratch += [pltpu.VMEM((2, 4, 4, 8, 2, 2, 32, 128), BF)]
    scratch += [pltpu.VMEM((288, 512), F32)] + [pltpu.VMEM((288, 512), BF)] * 4
    scratch += [pltpu.VMEM((288, 128), F32), pltpu.VMEM((2, 2, 144, 144), F32)]
    scratch += [pltpu.VMEM((PADC, 2 * PADC), F32), pltpu.VMEM((2, 2 * PADC, 128), F32)]
    scratch += [pltpu.VMEM((2, 640, 512), BF), pltpu.VMEM((4, 320, 512), BF)]
    scratch += [pltpu.VMEM((320, 1024), BF), pltpu.VMEM((2, 320, 1024), BF)]
    scratch += [pltpu.VMEM((320, 1024), BF), pltpu.VMEM((2, 640, 1024), BF)]
    scratch += [pltpu.VMEM((320, 1024), BF)] * 2 + [pltpu.VMEM((2, 640, 512), BF)]
    for shape in ((4, 3), (4, 3), (1,), (1,), (7,), (3,), (2,), (2,), (4,), (1,)):
        scratch += [dma(shape), dma(shape)]
    scratch += [dma((8,))]
    result = pl.pallas_call(
        kernel,
        out_shape=jax.ShapeDtypeStruct((2, 768, 512), BF),
        in_specs=[vmem] * (3 + len(early)) + [anywhere] * 8,
        out_specs=vmem,
        scratch_shapes=scratch,
        compiler_params=pltpu.CompilerParams(collective_id=0, has_side_effects=True, vmem_limit_bytes=60 * 2**20),
    )(*operands)
    return result.reshape(2, 4, 12, 16, 512)[:, :, :, :12]


def solution(mesh):
    return jax.shard_map(
        shards,
        mesh=mesh,
        in_specs=(
            P(None, None, "lat", "lon", None),
            P("lat"),
            P(),
            P(),
            P(),
            P(None, "lat", "lon"),
            P("lat", "lon"),
            P(),
        ),
        out_specs=P(None, None, "lat", "lon", None),
        check_vma=False,
    )
```

```python
import functools
import math

import jax
import jax.numpy as jnp
import numpy as np
from jax import lax
from jax.experimental import pallas as pl
from jax.experimental.pallas import tpu as pltpu
from jax.sharding import PartitionSpec as P

BF = jnp.bfloat16
F32 = jnp.float32
MESH = pl.DeviceIdType.MESH
EPSILON = 1e-05
NEG = -1e30
QSCALE = 32 ** (-0.5) * math.log2(math.e)

SEG = dict(A0=(0, 144), B0=(144, 288), A1=(288, 368), B1=(368, 448), C=(448, 528), D=(528, 608))
TOKENS = 608
REMOTE = ("B0", "B1", "C", "D")
UNIT = ((0, 288), (288, 608))
LEVELS = ((1, 2), (3, 0))
PADC = 80


def segment_row(level_index, r, c):
    east = c >= 6
    if 3 <= r < 9:
        name, rows, row = "A0" if east else "B0", 6, r - 3
    elif r >= 9:
        name, rows, row = "A1" if east else "B1", 3, r - 9
    else:
        name, rows, row = "C" if east else "D", 3, r
    return SEG[name][0] + (level_index * rows + row) * 6 + c % 6


def window_row(level_index, r, c):
    row = r - 3 if 3 <= r < 9 else (r - 9 if r >= 9 else r + 3)
    column = c - 6 if c >= 6 else c + 6
    return level_index * 72 + row * 12 + column


def coarse_row(level, row, column):
    return (level // 2) * PADC + (level % 2) * 36 + row * 6 + column


def tables():
    p1 = np.zeros((TOKENS, 576), np.float32)
    p2 = np.zeros((288, TOKENS), np.float32)
    p4 = np.zeros((4 * 2 * PADC, TOKENS), np.float32)
    p5 = np.zeros((576, 4 * 2 * PADC), np.float32)
    for r in range(12):
        for c in range(12):
            plane = (r % 2) + 2 * (c % 2)
            for index in range(4):
                level = LEVELS[index // 2][index % 2]
                seg = segment_row(index, r, c)
                place = (r * 12 + c) * 4 + level
                low = plane * 2 * PADC + coarse_row(level, r // 2, c // 2)
                p1[seg, place] = 1
                p2[window_row(index, r, c), seg] = 1
                p4[low, seg] = 1
                p5[place, low] = 1
    rows = np.zeros((2, 144, 32), np.float32)
    differ = np.zeros((144, 144), np.float32)
    level = np.zeros((144, 144), np.float32)
    for t in range(144):
        r6 = (t % 72) // 12
        rows[0, t, 3 + r6] = 1
        rows[1, t, 9 + r6 if r6 < 3 else 16 + r6 - 3] = 1
        for u in range(144):
            differ[t, u] = (r6 < 3) != ((u % 72) // 12 < 3)
            level[t, u] = (t // 72) != (u // 72)
    rows_t = np.zeros((2, 256, 144), np.float32)
    rows_t[:, 0:12] = rows.transpose(0, 2, 1)[:, 0:12]
    rows_t[:, 128:131] = rows.transpose(0, 2, 1)[:, 16:19]
    coarse = np.zeros((PADC, 16), np.float32)
    keep = np.zeros((2, 2 * PADC, 16), np.float32)
    for t in range(72):
        row = (t % 36) // 6
        coarse[t, 2 * row] = 1
        for group in range(2):
            for parity in range(2):
                keep[parity, group * PADC + t, 2 * row + parity] = 1
    coarse_t = np.zeros((128, 2 * PADC), np.float32)
    coarse_t[0:16, :PADC] = coarse.T
    coarse_t[0:16, PADC:] = coarse.T
    pads = np.zeros((8, 2 * PADC), np.float32)
    pads[:, np.arange(2 * PADC) % PADC >= 72] = 1
    ways = [p2[:, low:high] for low, high in UNIT]
    half = [p1, rows, rows_t, coarse, coarse_t, keep] + ways + [w.T.copy() for w in ways] + [p4, p5]
    return [jnp.asarray(a, BF) for a in half] + [jnp.asarray(a, F32) for a in (level, differ, pads)]


def dot(a, b):
    return jnp.dot(a, b, preferred_element_type=F32)


def dot_nt(a, b):
    return lax.dot_general(a, b, (((1,), (1,)), ((), ())), preferred_element_type=F32)


def normalised(x, width):
    mean = jnp.sum(x, axis=-1, keepdims=True) * (1.0 / width)
    centre = x - mean
    spread = jnp.sum(centre * centre, axis=-1, keepdims=True) * (1.0 / width)
    return centre * lax.rsqrt(spread + EPSILON)


def head_masks():
    head = lax.broadcasted_iota(jnp.int32, (16, 128), 1) // 32
    return [jnp.where(head == h, 1.0, 0.0).astype(BF)[0:1] for h in range(4)]


def weighed(expo, v4, mask):
    return dot(expo, jnp.concatenate([v4 * mask, jnp.broadcast_to(mask, v4.shape)], axis=1))


def attention(q4, k4, v4, bias, together):
    masks = head_masks()
    count = q4.shape[0]
    if together:
        scores = dot_nt(jnp.concatenate([q4 * m for m in masks], axis=0), k4)
    total = 0.0
    for h, mask in enumerate(masks):
        mine = (scores[h * count : (h + 1) * count] if together else dot_nt(q4 * mask, k4)) + bias
        expo = jnp.exp2(mine - jnp.max(mine, axis=-1, keepdims=True)).astype(BF)
        total = total + weighed(expo, v4, mask)
    return (total[:, :128] / total[:, 128:]).astype(BF)


def kernel(
    xp, vr, cqkv, cout, *rest
):
    tabs_h, (wqkv_h, wo_h, wm_h, we_h), out, rest = rest[:15], rest[15:19], rest[19], rest[20:]
    tabs, (wqkv, wo, wm, we), rest = rest[:15], rest[15:19], rest[19:]
    p1, r1, rt, rc, rct, rk, p2a, p2b, p3a, p3b, p4, p5, lm, dm, pads = tabs
    snd, xb, ret, zb, fl, fln, cw, pb, wg, xw, q, k, v, at, kcol, bias, cbias, krow, *rest = rest
    skp, nbm, mg, n2, q2, kv2, a2, co, dc, *rest = rest
    hs, hr, rs, rr, fs, fr, ps, pr, zs, zr, s2s, s2r, s3s, s3r, ds_, dr, ns, nr, ws = rest
    lat = lax.axis_index("lat")
    lon = lax.axis_index("lon")
    z, y_hi = lat // 2, lat % 2
    y_lo, x, c = lon // 8, (lon // 2) % 4, lon % 2
    y = y_hi * 2 + y_lo

    def device(z_, y_, x_, c_):
        return (z_ * 2 + y_ // 2, (y_ % 2) * 8 + x_ * 2 + c_)

    north, south = (lat + 15) % 16, (lat + 1) % 16
    west, east = (lon + 15) % 16, (lon + 1) % 16
    partner = device(z, y, x, 1 - c)

    barrier = pltpu.get_barrier_semaphore()
    greeted = [partner, (lat, west), (lat, east), (north, lon), (south, lon), (north, west), (south, east)]
    greeted += [device((z + d) % 8, y, x, c) for d in range(1, 8)]
    greeted += [device(z, (y + d) % 4, x, c) for d in range(1, 4)]
    greeted += [device(z, y, (x + d) % 4, c) for d in range(1, 4)]
    for target in greeted:
        pl.semaphore_signal(barrier, inc=1, device_id=target, device_id_type=MESH)

    order = list(range(15)) + [15, 16, 17, 18]
    pairs_ = list(zip(list(tabs_h) + [wqkv_h, wo_h, wm_h, we_h], list(tabs) + [wqkv, wo, wm, we]))
    loads = [pltpu.make_async_copy(*pairs_[n], ws.at[n]) for n in order]
    for n in (0, 1, 2, 3, 4, 5, 12, 13, 14, 6, 7, 15, 16, 8, 9, 10, 17, 18, 11):
        loads[n].start()

    def remote(src, dst, send, recv, target):
        return pltpu.make_async_remote_copy(
            src_ref=src, dst_ref=dst, send_sem=send, recv_sem=recv, device_id=target, device_id_type=MESH
        )

    def segments(source, target, send, recv, s, across_lon, across_lat, names):
        places = (("B0", (lat, across_lon)), ("B1", (lat, across_lon)), ("C", (across_lat, lon)), ("D", (across_lat, across_lon)))
        return [
            remote(source.at[s, slice(*SEG[name])], target.at[s, slice(*SEG[name])], send.at[s, n], recv.at[s, n], to)
            for n, (name, to) in enumerate(places)
            if name in names
        ]

    def halo(s, names=REMOTE):
        return segments(snd, xb, hs, hr, s, west, north, names)

    def back(s, names=REMOTE):
        return segments(ret, zb, rs, rr, s, east, south, names)

    flags = remote(fl, fln, fs.at[0], fr.at[0], (north, lon))
    pair = remote(cw, pb, ps.at[0], pr.at[0], partner)

    qkv_part, out_part = slice(0, 3), slice(3, 4)

    def along_z(n, m):
        block = wg.at[y_lo, x, m, z, y_hi, c]
        return [
            remote(block, block, zs.at[n, d - 1], zr.at[n, d - 1], device((z + d) % 8, y, x, c)) for d in range(1, 8)
        ]

    def second(n, m):
        block = wg.at[y_lo, x, m, :, y_hi, c]
        return [
            remote(block, block, s2s.at[n, d - 1], s2r.at[n, d - 1], device(z, (y + d * (1 - c)) % 4, (x + d * c) % 4, c))
            for d in range(1, 4)
        ]

    def chunk(core, step, m):
        if core == 0:
            return wg.at[:, (x + step) % 4, m, :, :, 0]
        other = (y + step) % 4
        return wg.at[other % 2, :, m, :, other // 2, 1]

    def ring(core, step):
        return device(z, y, (x + step) % 4, core) if core == 0 else device(z, (y + step) % 4, x, core)

    def third(core, m):
        block = chunk(core, 0, slice(m, m + 1))
        return [remote(block, block, s3s.at[m, d - 1], s3r.at[m, d - 1], ring(core, d)) for d in range(1, 4)]

    def across(core, m, d):
        block = chunk(core, (4 - d) % 4, slice(m, m + 1))
        return remote(block, block, ds_.at[m, d], dr.at[m, d], partner)

    def on_core(action):
        @pl.when(c == 0)
        def _():
            action(0)

        @pl.when(c == 1)
        def _():
            action(1)

    pl.semaphore_wait(barrier, len(greeted))
    place = lax.broadcasted_iota(jnp.int32, (64, 128), 1) == lax.broadcasted_iota(jnp.int32, (64, 128), 0) + 64 * c
    place = jnp.where(place, 1.0, 0.0).astype(BF)
    cw[0:3] = dot(cqkv[...].reshape(192, 64), place).astype(BF).reshape(3, 64, 128)
    cw[3] = dot(cout[...], place).astype(BF)
    pair.start()
    spread = jnp.where(
        lax.broadcasted_iota(jnp.int32, (12, 128), 1) == lax.broadcasted_iota(jnp.int32, (12, 128), 0), 1.0, 0.0
    )
    flat = dot(jnp.broadcast_to(vr[...].astype(F32), (16, 12)).astype(BF), spread.astype(BF))
    corner = lax.broadcasted_iota(jnp.int32, (16, 128), 1) == lax.broadcasted_iota(jnp.int32, (16, 128), 0)
    fl[16:32] = flat.astype(BF)
    fl[0:16] = dot(jnp.where(corner, flat, 0.0).astype(BF), jnp.ones((128, 128), BF)).astype(BF)
    flags.start()

    pair.wait_recv()
    block = cw[...] + pb[...]
    wg[y_lo, x, :, z, y_hi, c] = jnp.where(c == 0, block[:, :32], block[:, 32:])
    for copy in along_z(0, qkv_part):
        copy.start()

    loads[0].wait()
    for s in range(2):
        tokens = dot(p1[...], xp[s * 144 : (s + 1) * 144].reshape(576, 512)).astype(BF)
        snd[s] = tokens
        for name in ("A0", "A1"):
            xb[s, slice(*SEG[name])] = tokens[slice(*SEG[name])]
        for copy in halo(s):
            copy.start()

    def poll_z():
        for copy in along_z(0, qkv_part):
            copy.wait_recv()
        for copy in second(0, qkv_part) + along_z(1, out_part):
            copy.start()

    def poll_second():
        for copy in second(0, qkv_part) + along_z(1, out_part):
            copy.wait_recv()

        def go(core):
            for m in range(3):
                for copy in third(core, m):
                    copy.start()
            for m in range(3):
                across(core, m, 0).start()

        on_core(go)
        for copy in second(1, out_part):
            copy.start()

    def poll_third(m):
        def go(core):
            arrivals = third(core, m)
            for d in (1, 3, 2):
                arrivals[d - 1].wait_recv()
                across(core, m, d).start()

        on_core(go)

    def poll_out():
        for copy in second(1, out_part):
            copy.wait_recv()

        def go(core):
            for copy in third(core, 3) + [across(core, 3, 0)]:
                copy.start()

        on_core(go)

    def arrived(m):
        def go(core):
            for d in range(4):
                across(core, m, d).wait_recv()

        on_core(go)

    flags.wait_recv()
    for n in (1, 2, 3, 4, 5, 12, 13, 14):
        loads[n].wait()
    own, following = fl[...], fln[...]
    seam = jnp.where(lat == 15, NEG, 0.0)
    for w in range(2):
        down = dot(r1[w, :, 0:16], own[0:16]) + dot(r1[w, :, 16:32], following[0:16])
        flat = dot(own[16:32], rt[w, 0:128]) + dot(following[16:32], rt[w, 128:256])
        kcol[w * 144 : (w + 1) * 144] = down
        forbid = ((1.0 - flat[0:1]) * down[:, 0:1]) * NEG
        if w == 1:
            forbid = forbid + dm[...] * seam
        bias[0, w] = forbid
        bias[1, w] = forbid + lm[...] * NEG
    down = dot(rc[...], own[0:16])
    flat = dot(own[16:32], rct[...])
    cbias[...] = ((1.0 - flat[0:1]) * down[:, 0:1] + pads[0:1]) * NEG
    for parity in range(2):
        krow[parity] = dot(rk[parity], own[0:16])

    for n in (6, 7, 15, 16, 8, 9):
        loads[n].wait()

    def fine(s, w, after_qkv):
        for copy in halo(s, (("B0",), ("B1", "C", "D"))[w]):
            copy.wait_recv()
        low, high = UNIT[w]
        tokens = dot((p2a, p2b)[w][...], xb[s, low:high])
        xw[...] = tokens
        normed = normalised(tokens, 512).astype(BF)
        q[...] = (dot(normed, wqkv[:, 0:512]) * QSCALE).astype(BF)
        k[...] = dot(normed, wqkv[:, 512:1024]).astype(BF)
        v[...] = dot(normed, wqkv[:, 1024:1536]).astype(BF)
        after_qkv()
        for g in range(4):
            lanes = slice(g * 128, (g + 1) * 128)
            for group in range(2):
                rows = slice(group * 144, (group + 1) * 144)
                at[rows, lanes] = attention(q[rows, lanes], k[rows, lanes], v[rows, lanes], bias[group, w], False)
        keep = kcol[w * 144 : (w + 1) * 144, 0:1]
        skip = (xw[...] + dot(at[...], wo[...])).reshape(2, 144, 512) * keep[None]
        tokens = dot((p3a, p3b)[w][...], skip.reshape(288, 512).astype(BF)).astype(BF)
        ret[s, low:high] = tokens
        name = ("A0", "A1")[w]
        zb[s, slice(*SEG[name])] = tokens[slice(SEG[name][0] - low, SEG[name][1] - low)]
        for copy in back(s, (("B0",), ("B1", "C", "D"))[w]):
            copy.start()

    def nothing():
        return None

    fine(0, 0, poll_z)
    fine(0, 1, poll_second)
    fine(1, 1, nothing)
    fine(1, 0, nothing)
    for n in (10, 17, 18, 11):
        loads[n].wait()

    for s in range(2):
        for copy in back(s):
            copy.wait_recv()
        planes = dot(p4[...], zb[s])
        skp[s] = planes.astype(BF)
        planes = planes.reshape(4, 160, 512)
        mean = jnp.sum(jnp.sum(planes, axis=0), axis=-1, keepdims=True) * (1.0 / 2048)
        centre = planes - mean[None]
        spread = jnp.sum(jnp.sum(centre * centre, axis=0), axis=-1, keepdims=True) * (1.0 / 2048)
        nbm[:, s * 160 : (s + 1) * 160] = (centre * lax.rsqrt(spread + EPSILON)[None]).astype(BF)

    def merge(n, carry):
        lanes = pl.ds(pl.multiple_of(n * 256, 256), 256)
        total = dot(nbm[0], wm[0:512, lanes])
        for p in range(1, 4):
            total = total + dot(nbm[p], wm[512 * p : 512 * (p + 1), lanes])
        mg[:, lanes] = total.astype(BF)
        return carry

    lax.fori_loop(0, 4, merge, 0)
    n2[0] = normalised(mg[...].astype(F32), 1024).astype(BF)
    swap = remote(n2.at[0], n2.at[1], ns.at[0], nr.at[0], partner)
    swap.start()

    poll_third(0)
    poll_third(1)
    arrived(0)

    def weights(matrix, n):
        low = (n % 2) * 2
        pieces = [wg[n // 2, low + j, matrix].reshape(1024, 128) for j in range(2)]
        return jnp.concatenate(pieces, axis=1)

    def queries(n, carry):
        lanes = pl.ds(pl.multiple_of(n * 256, 256), 256)
        q2[:, lanes] = (dot(n2[0], weights(0, n)) * QSCALE).astype(BF)
        return carry

    lax.fori_loop(0, 4, queries, 0)
    poll_third(2)
    poll_out()
    swap.wait_recv()

    def keys(matrix, block, carry):
        lanes = pl.ds(pl.multiple_of(block * 256, 256), 256)
        kv2[matrix, :, lanes] = dot(n2[...].reshape(640, 1024), weights(matrix + 1, block)).astype(BF)
        return carry

    for matrix in range(2):
        arrived(1 + matrix)
        lax.fori_loop(0, 4, functools.partial(keys, matrix), 0)

    def heads(half, carry):
        for g in range(4):
            lanes = pl.ds(pl.multiple_of(half * 512 + g * 128, 128), 128)
            for j in range(4):
                rows, far = slice(j * PADC, (j + 1) * PADC), slice(320 + j * PADC, 320 + (j + 1) * PADC)
                k4 = jnp.concatenate([kv2[0, rows, lanes], kv2[0, far, lanes]], axis=0)
                v4 = jnp.concatenate([kv2[1, rows, lanes], kv2[1, far, lanes]], axis=0)
                a2[rows, lanes] = attention(q2[rows, lanes], k4, v4, cbias[...], True)
        return carry

    lax.fori_loop(0, 2, heads, 0)
    poll_third(3)
    arrived(3)

    def project(n, carry):
        lanes = pl.ds(pl.multiple_of(n * 256, 256), 256)
        co[:, lanes] = (mg[:, lanes].astype(F32) + dot(a2[...], weights(3, n))).astype(BF)
        return carry

    lax.fori_loop(0, 4, project, 0)

    def expand(n, carry):
        plane, side = n // 2, n % 2
        grown = dot(co[...], we[:, pl.ds(pl.multiple_of(n * 256, 256), 256)])
        rows = pl.ds(pl.multiple_of(plane * 160, 160), 160)
        lanes = pl.ds(pl.multiple_of(side * 256, 256), 256)
        keep = krow[plane % 2][:, 0:1]
        for s in range(2):
            dc[s, rows, lanes] = ((skp[s, rows, lanes].astype(F32) + grown[s * 160 : (s + 1) * 160]) * keep).astype(BF)
        return carry

    lax.fori_loop(0, 8, expand, 0)
    for s in range(2):
        out[s * 144 : (s + 1) * 144] = dot(p5[...], dc[s]).astype(BF).reshape(144, 4, 512)

    pair.wait_send()
    flags.wait_send()
    swap.wait_send()
    for s in range(2):
        for copy in halo(s) + back(s):
            copy.wait_send()
    for n, m in enumerate((qkv_part, out_part)):
        for copy in along_z(n, m) + second(n, m):
            copy.wait_send()

    def go(core):
        for m in range(4):
            for copy in third(core, m) + [across(core, m, d) for d in range(4)]:
                copy.wait_send()

    on_core(go)


def shards(fields, valid_rows, fine_qkv, fine_out, merge_weight, coarse_qkv, coarse_out, expand_weight):
    tabs = tables()
    xp = fields.transpose(0, 2, 3, 1, 4).reshape(288, 4, 512)
    operands = [xp, valid_rows.reshape(1, 12), coarse_qkv, coarse_out] + tabs
    operands += [fine_qkv, fine_out, merge_weight, expand_weight]
    vmem = pl.BlockSpec(memory_space=pltpu.VMEM)
    anywhere = pl.BlockSpec(memory_space=pl.ANY)
    dma = pltpu.SemaphoreType.DMA
    scratch = [pltpu.VMEM(a.shape, a.dtype) for a in tabs]
    scratch += [pltpu.VMEM(a.shape, BF) for a in (fine_qkv, fine_out, merge_weight, expand_weight)]
    scratch += [pltpu.VMEM((2, TOKENS, 512), BF)] * 4
    scratch += [pltpu.VMEM((32, 128), BF)] * 2 + [pltpu.VMEM((4, 64, 128), BF)] * 2
    scratch += [pltpu.VMEM((2, 4, 4, 8, 2, 2, 32, 128), BF)]
    scratch += [pltpu.VMEM((288, 512), F32)] + [pltpu.VMEM((288, 512), BF)] * 4
    scratch += [pltpu.VMEM((288, 128), F32), pltpu.VMEM((2, 2, 144, 144), F32)]
    scratch += [pltpu.VMEM((PADC, 2 * PADC), F32), pltpu.VMEM((2, 2 * PADC, 128), F32)]
    scratch += [pltpu.VMEM((2, 640, 512), BF), pltpu.VMEM((4, 320, 512), BF)]
    scratch += [pltpu.VMEM((320, 1024), BF), pltpu.VMEM((2, 320, 1024), BF)]
    scratch += [pltpu.VMEM((320, 1024), BF), pltpu.VMEM((2, 640, 1024), BF)]
    scratch += [pltpu.VMEM((320, 1024), BF)] * 2 + [pltpu.VMEM((2, 640, 512), BF)]
    for shape in ((2, 4), (2, 4), (1,), (1,), (2, 7), (2, 3), (4, 3), (4, 4), (1,)):
        scratch += [dma(shape), dma(shape)]
    scratch += [dma((19,))]
    result = pl.pallas_call(
        kernel,
        out_shape=jax.ShapeDtypeStruct((288, 4, 512), BF),
        in_specs=[vmem] * 4 + [anywhere] * 19,
        out_specs=vmem,
        scratch_shapes=scratch,
        compiler_params=pltpu.CompilerParams(collective_id=0, has_side_effects=True, vmem_limit_bytes=60 * 2**20),
    )(*operands)
    return result.reshape(2, 12, 12, 4, 512).transpose(0, 3, 1, 2, 4)


def solution(mesh):
    return jax.shard_map(
        shards,
        mesh=mesh,
        in_specs=(
            P(None, None, "lat", "lon", None),
            P("lat"),
            P(),
            P(),
            P(),
            P(None, "lat", "lon"),
            P("lat", "lon"),
            P(),
        ),
        out_specs=P(None, None, "lat", "lon", None),
        check_vma=False,
    )
```

```python
import functools
import math

import jax
import jax.numpy as jnp
import numpy as np
from jax import lax
from jax.experimental import pallas as pl
from jax.experimental.pallas import tpu as pltpu
from jax.sharding import PartitionSpec as P

BF = jnp.bfloat16
F32 = jnp.float32
MESH = pl.DeviceIdType.MESH
EPSILON = 1e-05
NEG = -1e30
QSCALE = 32 ** (-0.5) * math.log2(math.e)

SEG = dict(A0=(0, 144), B0=(144, 288), A1=(288, 368), B1=(368, 448), C=(448, 528), D=(528, 608))
TOKENS = 608
REMOTE = ("B0", "B1", "C", "D")
UNIT = ((0, 288), (288, 608))
LEVELS = ((1, 2), (3, 0))
PADC = 80


def segment_row(level_index, r, c):
    east = c >= 6
    if 3 <= r < 9:
        name, rows, row = "A0" if east else "B0", 6, r - 3
    elif r >= 9:
        name, rows, row = "A1" if east else "B1", 3, r - 9
    else:
        name, rows, row = "C" if east else "D", 3, r
    return SEG[name][0] + (level_index * rows + row) * 6 + c % 6


def window_row(level_index, r, c):
    row = r - 3 if 3 <= r < 9 else (r - 9 if r >= 9 else r + 3)
    column = c - 6 if c >= 6 else c + 6
    return level_index * 72 + row * 12 + column


def coarse_row(level, row, column):
    return (level // 2) * PADC + (level % 2) * 36 + row * 6 + column


def tables():
    p1 = np.zeros((TOKENS, 576), np.float32)
    p2 = np.zeros((288, TOKENS), np.float32)
    p4 = np.zeros((4 * 2 * PADC, TOKENS), np.float32)
    p5 = np.zeros((576, 4 * 2 * PADC), np.float32)
    for r in range(12):
        for c in range(12):
            plane = (r % 2) + 2 * (c % 2)
            for index in range(4):
                level = LEVELS[index // 2][index % 2]
                seg = segment_row(index, r, c)
                place = (r * 12 + c) * 4 + level
                low = plane * 2 * PADC + coarse_row(level, r // 2, c // 2)
                p1[seg, place] = 1
                p2[window_row(index, r, c), seg] = 1
                p4[low, seg] = 1
                p5[place, low] = 1
    rows = np.zeros((2, 144, 32), np.float32)
    differ = np.zeros((144, 144), np.float32)
    level = np.zeros((144, 144), np.float32)
    for t in range(144):
        r6 = (t % 72) // 12
        rows[0, t, 3 + r6] = 1
        rows[1, t, 9 + r6 if r6 < 3 else 16 + r6 - 3] = 1
        for u in range(144):
            differ[t, u] = (r6 < 3) != ((u % 72) // 12 < 3)
            level[t, u] = (t // 72) != (u // 72)
    rows_t = np.zeros((2, 256, 144), np.float32)
    rows_t[:, 0:12] = rows.transpose(0, 2, 1)[:, 0:12]
    rows_t[:, 128:131] = rows.transpose(0, 2, 1)[:, 16:19]
    coarse = np.zeros((PADC, 16), np.float32)
    keep = np.zeros((2, 2 * PADC, 16), np.float32)
    for t in range(72):
        row = (t % 36) // 6
        coarse[t, 2 * row] = 1
        for group in range(2):
            for parity in range(2):
                keep[parity, group * PADC + t, 2 * row + parity] = 1
    coarse_t = np.zeros((128, 2 * PADC), np.float32)
    coarse_t[0:16, :PADC] = coarse.T
    coarse_t[0:16, PADC:] = coarse.T
    pads = np.zeros((8, 2 * PADC), np.float32)
    pads[:, np.arange(2 * PADC) % PADC >= 72] = 1
    ways = [p2[:, low:high] for low, high in UNIT]
    half = [p1, rows, rows_t, coarse, coarse_t, keep] + ways + [w.T.copy() for w in ways] + [p4, p5]
    return [jnp.asarray(a, BF) for a in half] + [jnp.asarray(a, F32) for a in (level, differ, pads)]


def dot(a, b):
    return jnp.dot(a, b, preferred_element_type=F32)


def dot_nt(a, b):
    return lax.dot_general(a, b, (((1,), (1,)), ((), ())), preferred_element_type=F32)


def normalised(x, width):
    mean = jnp.sum(x, axis=-1, keepdims=True) * (1.0 / width)
    centre = x - mean
    spread = jnp.sum(centre * centre, axis=-1, keepdims=True) * (1.0 / width)
    return centre * lax.rsqrt(spread + EPSILON)


def head_masks():
    head = lax.broadcasted_iota(jnp.int32, (16, 128), 1) // 32
    return [jnp.where(head == h, 1.0, 0.0).astype(BF)[0:1] for h in range(4)]


def weighed(expo, v4, mask):
    return dot(expo, jnp.concatenate([v4 * mask, jnp.broadcast_to(mask, v4.shape)], axis=1))


def attention(q4, k4, v4, bias, together):
    masks = head_masks()
    count = q4.shape[0]
    if together:
        scores = dot_nt(jnp.concatenate([q4 * m for m in masks], axis=0), k4)
    total = 0.0
    for h, mask in enumerate(masks):
        mine = (scores[h * count : (h + 1) * count] if together else dot_nt(q4 * mask, k4)) + bias
        expo = jnp.exp2(mine - jnp.max(mine, axis=-1, keepdims=True)).astype(BF)
        total = total + weighed(expo, v4, mask)
    return (total[:, :128] / total[:, 128:]).astype(BF)


def kernel(
    xp, vr, cqkv, cout, *rest
):
    tabs_h, (wqkv_h, wo_h, wm_h, we_h), out, rest = rest[:15], rest[15:19], rest[19], rest[20:]
    tabs, (wqkv, wo, wm, we), rest = rest[:15], rest[15:19], rest[19:]
    p1, r1, rt, rc, rct, rk, p2a, p2b, p3a, p3b, p4, p5, lm, dm, pads = tabs
    snd, xb, ret, zb, fl, fln, cw, pb, wg, xw, q, k, v, at, kcol, bias, cbias, krow, *rest = rest
    skp, nbm, mg, n2, q2, kv2, a2, co, dc, *rest = rest
    hs, hr, rs, rr, fs, fr, ps, pr, zs, zr, s2s, s2r, s3s, s3r, ds_, dr, ns, nr, ws = rest
    lat = lax.axis_index("lat")
    lon = lax.axis_index("lon")
    z, y_hi = lat // 2, lat % 2
    y_lo, x, c = lon // 8, (lon // 2) % 4, lon % 2
    y = y_hi * 2 + y_lo

    def device(z_, y_, x_, c_):
        return (z_ * 2 + y_ // 2, (y_ % 2) * 8 + x_ * 2 + c_)

    north, south = (lat + 15) % 16, (lat + 1) % 16
    west, east = (lon + 15) % 16, (lon + 1) % 16
    partner = device(z, y, x, 1 - c)

    barrier = pltpu.get_barrier_semaphore()
    greeted = [partner, (lat, west), (lat, east), (north, lon), (south, lon), (north, west), (south, east)]
    greeted += [device((z + d) % 8, y, x, c) for d in range(1, 8)]
    greeted += [device(z, (y + d) % 4, x, c) for d in range(1, 4)]
    greeted += [device(z, y, (x + d) % 4, c) for d in range(1, 4)]
    for target in greeted:
        pl.semaphore_signal(barrier, inc=1, device_id=target, device_id_type=MESH)

    order = list(range(15)) + [15, 16, 17, 18]
    pairs_ = list(zip(list(tabs_h) + [wqkv_h, wo_h, wm_h, we_h], list(tabs) + [wqkv, wo, wm, we]))
    loads = [pltpu.make_async_copy(*pairs_[n], ws.at[n]) for n in order]
    for n in (0, 1, 2, 3, 4, 5, 12, 13, 14, 6, 7, 15, 16, 8, 9, 10, 17, 18, 11):
        loads[n].start()

    def remote(src, dst, send, recv, target):
        return pltpu.make_async_remote_copy(
            src_ref=src, dst_ref=dst, send_sem=send, recv_sem=recv, device_id=target, device_id_type=MESH
        )

    def segments(source, target, send, recv, s, across_lon, across_lat, names):
        places = (("B0", (lat, across_lon)), ("B1", (lat, across_lon)), ("C", (across_lat, lon)), ("D", (across_lat, across_lon)))
        return [
            remote(source.at[s, slice(*SEG[name])], target.at[s, slice(*SEG[name])], send.at[s, n], recv.at[s, n], to)
            for n, (name, to) in enumerate(places)
            if name in names
        ]

    def halo(s, names=REMOTE):
        return segments(snd, xb, hs, hr, s, west, north, names)

    def back(s, names=REMOTE):
        return segments(ret, zb, rs, rr, s, east, south, names)

    flags = remote(fl, fln, fs.at[0], fr.at[0], (north, lon))
    pair = remote(cw, pb, ps.at[0], pr.at[0], partner)

    def first():
        block = wg.at[y_lo, x, :, z, y_hi, c]
        return [
            remote(block, block, s2s.at[d - 1], s2r.at[d - 1], device(z, (y + d * (1 - c)) % 4, (x + d * c) % 4, c))
            for d in range(1, 4)
        ]

    def along_z(core, m):
        block = wg.at[:, x, m, z, :, 0] if core == 0 else wg.at[y_lo, :, m, z, y_hi, 1]
        return [
            remote(block, block, zs.at[m, d - 1], zr.at[m, d - 1], device((z + d) % 8, y, x, core)) for d in range(1, 8)
        ]

    def chunk(core, step, m):
        if core == 0:
            return wg.at[:, (x + step) % 4, m, :, :, 0]
        other = (y + step) % 4
        return wg.at[other % 2, :, m, :, other // 2, 1]

    def ring(core, step):
        return device(z, y, (x + step) % 4, core) if core == 0 else device(z, (y + step) % 4, x, core)

    def third(core, m):
        block = chunk(core, 0, slice(m, m + 1))
        return [remote(block, block, s3s.at[m, d - 1], s3r.at[m, d - 1], ring(core, d)) for d in range(1, 4)]

    def across(core, m, d):
        block = chunk(core, (4 - d) % 4, slice(m, m + 1))
        return remote(block, block, ds_.at[m, d], dr.at[m, d], partner)

    def on_core(action):
        @pl.when(c == 0)
        def _():
            action(0)

        @pl.when(c == 1)
        def _():
            action(1)

    pl.semaphore_wait(barrier, len(greeted))
    place = lax.broadcasted_iota(jnp.int32, (64, 128), 1) == lax.broadcasted_iota(jnp.int32, (64, 128), 0) + 64 * c
    place = jnp.where(place, 1.0, 0.0).astype(BF)
    cw[0:3] = dot(cqkv[...].reshape(192, 64), place).astype(BF).reshape(3, 64, 128)
    cw[3] = dot(cout[...], place).astype(BF)
    pair.start()
    spread = jnp.where(
        lax.broadcasted_iota(jnp.int32, (12, 128), 1) == lax.broadcasted_iota(jnp.int32, (12, 128), 0), 1.0, 0.0
    )
    flat = dot(jnp.broadcast_to(vr[...].astype(F32), (16, 12)).astype(BF), spread.astype(BF))
    corner = lax.broadcasted_iota(jnp.int32, (16, 128), 1) == lax.broadcasted_iota(jnp.int32, (16, 128), 0)
    fl[16:32] = flat.astype(BF)
    fl[0:16] = dot(jnp.where(corner, flat, 0.0).astype(BF), jnp.ones((128, 128), BF)).astype(BF)
    flags.start()

    pair.wait_recv()
    block = cw[...] + pb[...]
    wg[y_lo, x, :, z, y_hi, c] = jnp.where(c == 0, block[:, :32], block[:, 32:])
    for copy in first():
        copy.start()

    loads[0].wait()
    for s in range(2):
        tokens = dot(p1[...], xp[s * 144 : (s + 1) * 144].reshape(576, 512)).astype(BF)
        snd[s] = tokens
        for name in ("A0", "A1"):
            xb[s, slice(*SEG[name])] = tokens[slice(*SEG[name])]
        for copy in halo(s):
            copy.start()

    def poll_first():
        for copy in first():
            copy.wait_recv()

        def go(core):
            for m in range(2):
                for copy in along_z(core, m):
                    copy.start()

        on_core(go)

    def poll_z(m):
        def go(core):
            for copy in along_z(core, m):
                copy.wait_recv()
            later = along_z(core, m + 2) if m + 2 < 4 else []
            for copy in third(core, m) + [across(core, m, 0)] + later:
                copy.start()

        on_core(go)

    def poll_third(m):
        def go(core):
            arrivals = third(core, m)
            for d in (1, 3, 2):
                arrivals[d - 1].wait_recv()
                across(core, m, d).start()

        on_core(go)

    def arrived(m):
        def go(core):
            for d in range(4):
                across(core, m, d).wait_recv()

        on_core(go)

    poll_first()

    flags.wait_recv()
    for n in (1, 2, 3, 4, 5, 12, 13, 14):
        loads[n].wait()
    own, following = fl[...], fln[...]
    seam = jnp.where(lat == 15, NEG, 0.0)
    for w in range(2):
        down = dot(r1[w, :, 0:16], own[0:16]) + dot(r1[w, :, 16:32], following[0:16])
        flat = dot(own[16:32], rt[w, 0:128]) + dot(following[16:32], rt[w, 128:256])
        kcol[w * 144 : (w + 1) * 144] = down
        forbid = ((1.0 - flat[0:1]) * down[:, 0:1]) * NEG
        if w == 1:
            forbid = forbid + dm[...] * seam
        bias[0, w] = forbid
        bias[1, w] = forbid + lm[...] * NEG
    down = dot(rc[...], own[0:16])
    flat = dot(own[16:32], rct[...])
    cbias[...] = ((1.0 - flat[0:1]) * down[:, 0:1] + pads[0:1]) * NEG
    for parity in range(2):
        krow[parity] = dot(rk[parity], own[0:16])

    for n in (6, 7, 15, 16, 8, 9):
        loads[n].wait()

    def fine(s, w, after_qkv):
        for copy in halo(s, (("B0",), ("B1", "C", "D"))[w]):
            copy.wait_recv()
        low, high = UNIT[w]
        tokens = dot((p2a, p2b)[w][...], xb[s, low:high])
        xw[...] = tokens
        normed = normalised(tokens, 512).astype(BF)
        q[...] = (dot(normed, wqkv[:, 0:512]) * QSCALE).astype(BF)
        k[...] = dot(normed, wqkv[:, 512:1024]).astype(BF)
        v[...] = dot(normed, wqkv[:, 1024:1536]).astype(BF)
        after_qkv()
        for g in range(4):
            lanes = slice(g * 128, (g + 1) * 128)
            for group in range(2):
                rows = slice(group * 144, (group + 1) * 144)
                at[rows, lanes] = attention(q[rows, lanes], k[rows, lanes], v[rows, lanes], bias[group, w], False)
        keep = kcol[w * 144 : (w + 1) * 144, 0:1]
        skip = (xw[...] + dot(at[...], wo[...])).reshape(2, 144, 512) * keep[None]
        tokens = dot((p3a, p3b)[w][...], skip.reshape(288, 512).astype(BF)).astype(BF)
        ret[s, low:high] = tokens
        name = ("A0", "A1")[w]
        zb[s, slice(*SEG[name])] = tokens[slice(SEG[name][0] - low, SEG[name][1] - low)]
        for copy in back(s, (("B0",), ("B1", "C", "D"))[w]):
            copy.start()

    def nothing():
        return None

    fine(0, 0, nothing)
    fine(0, 1, nothing)
    fine(1, 1, nothing)
    poll_z(0)
    fine(1, 0, nothing)
    poll_z(1)
    poll_z(2)
    for n in (10, 17, 18, 11):
        loads[n].wait()

    for s in range(2):
        for copy in back(s):
            copy.wait_recv()
        planes = dot(p4[...], zb[s])
        skp[s] = planes.astype(BF)
        planes = planes.reshape(4, 160, 512)
        mean = jnp.sum(jnp.sum(planes, axis=0), axis=-1, keepdims=True) * (1.0 / 2048)
        centre = planes - mean[None]
        spread = jnp.sum(jnp.sum(centre * centre, axis=0), axis=-1, keepdims=True) * (1.0 / 2048)
        nbm[:, s * 160 : (s + 1) * 160] = (centre * lax.rsqrt(spread + EPSILON)[None]).astype(BF)

    def merge(n, carry):
        lanes = pl.ds(pl.multiple_of(n * 256, 256), 256)
        total = dot(nbm[0], wm[0:512, lanes])
        for p in range(1, 4):
            total = total + dot(nbm[p], wm[512 * p : 512 * (p + 1), lanes])
        mg[:, lanes] = total.astype(BF)
        return carry

    lax.fori_loop(0, 4, merge, 0)
    n2[0] = normalised(mg[...].astype(F32), 1024).astype(BF)
    swap = remote(n2.at[0], n2.at[1], ns.at[0], nr.at[0], partner)
    swap.start()

    poll_third(0)
    poll_third(1)
    arrived(0)

    def weights(matrix, n):
        low = (n % 2) * 2
        pieces = [wg[n // 2, low + j, matrix].reshape(1024, 128) for j in range(2)]
        return jnp.concatenate(pieces, axis=1)

    def queries(n, carry):
        lanes = pl.ds(pl.multiple_of(n * 256, 256), 256)
        q2[:, lanes] = (dot(n2[0], weights(0, n)) * QSCALE).astype(BF)
        return carry

    lax.fori_loop(0, 4, queries, 0)
    poll_third(2)
    poll_z(3)
    swap.wait_recv()

    def keys(matrix, block, carry):
        lanes = pl.ds(pl.multiple_of(block * 256, 256), 256)
        kv2[matrix, :, lanes] = dot(n2[...].reshape(640, 1024), weights(matrix + 1, block)).astype(BF)
        return carry

    for matrix in range(2):
        arrived(1 + matrix)
        lax.fori_loop(0, 4, functools.partial(keys, matrix), 0)

    def heads(half, carry):
        for g in range(4):
            lanes = pl.ds(pl.multiple_of(half * 512 + g * 128, 128), 128)
            for j in range(4):
                rows, far = slice(j * PADC, (j + 1) * PADC), slice(320 + j * PADC, 320 + (j + 1) * PADC)
                k4 = jnp.concatenate([kv2[0, rows, lanes], kv2[0, far, lanes]], axis=0)
                v4 = jnp.concatenate([kv2[1, rows, lanes], kv2[1, far, lanes]], axis=0)
                a2[rows, lanes] = attention(q2[rows, lanes], k4, v4, cbias[...], True)
        return carry

    lax.fori_loop(0, 2, heads, 0)
    poll_third(3)
    arrived(3)

    def project(n, carry):
        lanes = pl.ds(pl.multiple_of(n * 256, 256), 256)
        co[:, lanes] = (mg[:, lanes].astype(F32) + dot(a2[...], weights(3, n))).astype(BF)
        return carry

    lax.fori_loop(0, 4, project, 0)

    def expand(n, carry):
        plane, side = n // 2, n % 2
        grown = dot(co[...], we[:, pl.ds(pl.multiple_of(n * 256, 256), 256)])
        rows = pl.ds(pl.multiple_of(plane * 160, 160), 160)
        lanes = pl.ds(pl.multiple_of(side * 256, 256), 256)
        keep = krow[plane % 2][:, 0:1]
        for s in range(2):
            dc[s, rows, lanes] = ((skp[s, rows, lanes].astype(F32) + grown[s * 160 : (s + 1) * 160]) * keep).astype(BF)
        return carry

    lax.fori_loop(0, 8, expand, 0)
    for s in range(2):
        out[s * 144 : (s + 1) * 144] = dot(p5[...], dc[s]).astype(BF).reshape(144, 4, 512)

    pair.wait_send()
    flags.wait_send()
    swap.wait_send()
    for s in range(2):
        for copy in halo(s) + back(s):
            copy.wait_send()
    for copy in first():
        copy.wait_send()

    def go(core):
        for m in range(4):
            for copy in along_z(core, m) + third(core, m) + [across(core, m, d) for d in range(4)]:
                copy.wait_send()

    on_core(go)


def shards(fields, valid_rows, fine_qkv, fine_out, merge_weight, coarse_qkv, coarse_out, expand_weight):
    tabs = tables()
    xp = fields.transpose(0, 2, 3, 1, 4).reshape(288, 4, 512)
    operands = [xp, valid_rows.reshape(1, 12), coarse_qkv, coarse_out] + tabs
    operands += [fine_qkv, fine_out, merge_weight, expand_weight]
    vmem = pl.BlockSpec(memory_space=pltpu.VMEM)
    anywhere = pl.BlockSpec(memory_space=pl.ANY)
    dma = pltpu.SemaphoreType.DMA
    scratch = [pltpu.VMEM(a.shape, a.dtype) for a in tabs]
    scratch += [pltpu.VMEM(a.shape, BF) for a in (fine_qkv, fine_out, merge_weight, expand_weight)]
    scratch += [pltpu.VMEM((2, TOKENS, 512), BF)] * 4
    scratch += [pltpu.VMEM((32, 128), BF)] * 2 + [pltpu.VMEM((4, 64, 128), BF)] * 2
    scratch += [pltpu.VMEM((2, 4, 4, 8, 2, 2, 32, 128), BF)]
    scratch += [pltpu.VMEM((288, 512), F32)] + [pltpu.VMEM((288, 512), BF)] * 4
    scratch += [pltpu.VMEM((288, 128), F32), pltpu.VMEM((2, 2, 144, 144), F32)]
    scratch += [pltpu.VMEM((PADC, 2 * PADC), F32), pltpu.VMEM((2, 2 * PADC, 128), F32)]
    scratch += [pltpu.VMEM((2, 640, 512), BF), pltpu.VMEM((4, 320, 512), BF)]
    scratch += [pltpu.VMEM((320, 1024), BF), pltpu.VMEM((2, 320, 1024), BF)]
    scratch += [pltpu.VMEM((320, 1024), BF), pltpu.VMEM((2, 640, 1024), BF)]
    scratch += [pltpu.VMEM((320, 1024), BF)] * 2 + [pltpu.VMEM((2, 640, 512), BF)]
    for shape in ((2, 4), (2, 4), (1,), (1,), (4, 7), (3,), (4, 3), (4, 4), (1,)):
        scratch += [dma(shape), dma(shape)]
    scratch += [dma((19,))]
    result = pl.pallas_call(
        kernel,
        out_shape=jax.ShapeDtypeStruct((288, 4, 512), BF),
        in_specs=[vmem] * 4 + [anywhere] * 19,
        out_specs=vmem,
        scratch_shapes=scratch,
        compiler_params=pltpu.CompilerParams(collective_id=0, has_side_effects=True, vmem_limit_bytes=60 * 2**20),
    )(*operands)
    return result.reshape(2, 12, 12, 4, 512).transpose(0, 3, 1, 2, 4)


def solution(mesh):
    return jax.shard_map(
        shards,
        mesh=mesh,
        in_specs=(
            P(None, None, "lat", "lon", None),
            P("lat"),
            P(),
            P(),
            P(),
            P(None, "lat", "lon"),
            P("lat", "lon"),
            P(),
        ),
        out_specs=P(None, None, "lat", "lon", None),
        check_vma=False,
    )
```

```python
import functools
import math

import jax
import jax.numpy as jnp
import numpy as np
from jax import lax
from jax.experimental import pallas as pl
from jax.experimental.pallas import tpu as pltpu
from jax.sharding import PartitionSpec as P

BF = jnp.bfloat16
F32 = jnp.float32
MESH = pl.DeviceIdType.MESH
EPSILON = 1e-05
NEG = -1e30
QSCALE = 32 ** (-0.5) * math.log2(math.e)

SEG = dict(A0=(0, 144), B0=(144, 288), A1=(288, 368), B1=(368, 448), C=(448, 528), D=(528, 608))
TOKENS = 608
REMOTE = ("B0", "B1", "C", "D")
UNIT = ((0, 288), (288, 608))
LEVELS = ((1, 2), (3, 0))
PADC = 80


def segment_row(level_index, r, c):
    east = c >= 6
    if 3 <= r < 9:
        name, rows, row = "A0" if east else "B0", 6, r - 3
    elif r >= 9:
        name, rows, row = "A1" if east else "B1", 3, r - 9
    else:
        name, rows, row = "C" if east else "D", 3, r
    return SEG[name][0] + (level_index * rows + row) * 6 + c % 6


def window_row(level_index, r, c):
    row = r - 3 if 3 <= r < 9 else (r - 9 if r >= 9 else r + 3)
    column = c - 6 if c >= 6 else c + 6
    return level_index * 72 + row * 12 + column


def coarse_row(level, row, column):
    return (level // 2) * PADC + (level % 2) * 36 + row * 6 + column


def tables():
    p1 = np.zeros((TOKENS, 576), np.float32)
    p2 = np.zeros((288, TOKENS), np.float32)
    p4 = np.zeros((4 * 2 * PADC, TOKENS), np.float32)
    p5 = np.zeros((576, 4 * 2 * PADC), np.float32)
    for r in range(12):
        for c in range(12):
            plane = (r % 2) + 2 * (c % 2)
            for index in range(4):
                level = LEVELS[index // 2][index % 2]
                seg = segment_row(index, r, c)
                place = (r * 12 + c) * 4 + level
                low = plane * 2 * PADC + coarse_row(level, r // 2, c // 2)
                p1[seg, place] = 1
                p2[window_row(index, r, c), seg] = 1
                p4[low, seg] = 1
                p5[place, low] = 1
    rows = np.zeros((2, 144, 32), np.float32)
    differ = np.zeros((144, 144), np.float32)
    level = np.zeros((144, 144), np.float32)
    for t in range(144):
        r6 = (t % 72) // 12
        rows[0, t, 3 + r6] = 1
        rows[1, t, 9 + r6 if r6 < 3 else 16 + r6 - 3] = 1
        for u in range(144):
            differ[t, u] = (r6 < 3) != ((u % 72) // 12 < 3)
            level[t, u] = (t // 72) != (u // 72)
    rows_t = np.zeros((2, 256, 144), np.float32)
    rows_t[:, 0:12] = rows.transpose(0, 2, 1)[:, 0:12]
    rows_t[:, 128:131] = rows.transpose(0, 2, 1)[:, 16:19]
    coarse = np.zeros((PADC, 16), np.float32)
    keep = np.zeros((2, 2 * PADC, 16), np.float32)
    for t in range(72):
        row = (t % 36) // 6
        coarse[t, 2 * row] = 1
        for group in range(2):
            for parity in range(2):
                keep[parity, group * PADC + t, 2 * row + parity] = 1
    coarse_t = np.zeros((128, 2 * PADC), np.float32)
    coarse_t[0:16, :PADC] = coarse.T
    coarse_t[0:16, PADC:] = coarse.T
    pads = np.zeros((8, 2 * PADC), np.float32)
    pads[:, np.arange(2 * PADC) % PADC >= 72] = 1
    ways = [p2[:, low:high] for low, high in UNIT]
    half = [p1, rows, rows_t, coarse, coarse_t, keep] + ways + [w.T.copy() for w in ways] + [p4, p5]
    return [jnp.asarray(a, BF) for a in half] + [jnp.asarray(a, F32) for a in (level, differ, pads)]


def dot(a, b):
    return jnp.dot(a, b, preferred_element_type=F32)


def dot_nt(a, b):
    return lax.dot_general(a, b, (((1,), (1,)), ((), ())), preferred_element_type=F32)


def normalised(x, width):
    mean = jnp.sum(x, axis=-1, keepdims=True) * (1.0 / width)
    centre = x - mean
    spread = jnp.sum(centre * centre, axis=-1, keepdims=True) * (1.0 / width)
    return centre * lax.rsqrt(spread + EPSILON)


def head_masks():
    head = lax.broadcasted_iota(jnp.int32, (16, 128), 1) // 32
    return [jnp.where(head == h, 1.0, 0.0).astype(BF)[0:1] for h in range(4)]


def weighed(expo, v4, mask):
    return dot(expo, jnp.concatenate([v4 * mask, jnp.broadcast_to(mask, v4.shape)], axis=1))


def attention(q4, k4, v4, bias, together):
    masks = head_masks()
    count = q4.shape[0]
    if together:
        scores = dot_nt(jnp.concatenate([q4 * m for m in masks], axis=0), k4)
    total = 0.0
    for h, mask in enumerate(masks):
        mine = (scores[h * count : (h + 1) * count] if together else dot_nt(q4 * mask, k4)) + bias
        expo = jnp.exp2(mine - jnp.max(mine, axis=-1, keepdims=True)).astype(BF)
        total = total + weighed(expo, v4, mask)
    return (total[:, :128] / total[:, 128:]).astype(BF)


def kernel(
    xp, vr, cqkv, cout, *rest
):
    tabs_h, (wqkv_h, wo_h, wm_h, we_h), out, rest = rest[:15], rest[15:19], rest[19], rest[20:]
    tabs, (wqkv, wo, wm, we), rest = rest[:15], rest[15:19], rest[19:]
    p1, r1, rt, rc, rct, rk, p2a, p2b, p3a, p3b, p4, p5, lm, dm, pads = tabs
    snd, xb, ret, zb, fl, fln, cw, pb, wg, xw, q, k, v, at, kcol, bias, cbias, krow, *rest = rest
    skp, nbm, mg, n2, q2, kv2, a2, co, dc, *rest = rest
    hs, hr, rs, rr, fs, fr, ps, pr, zs, zr, s2s, s2r, s3s, s3r, ds_, dr, ns, nr, ws = rest
    lat = lax.axis_index("lat")
    lon = lax.axis_index("lon")
    z, y_hi = lat // 2, lat % 2
    y_lo, x, c = lon // 8, (lon // 2) % 4, lon % 2
    y = y_hi * 2 + y_lo

    def device(z_, y_, x_, c_):
        return (z_ * 2 + y_ // 2, (y_ % 2) * 8 + x_ * 2 + c_)

    north, south = (lat + 15) % 16, (lat + 1) % 16
    west, east = (lon + 15) % 16, (lon + 1) % 16
    partner = device(z, y, x, 1 - c)

    barrier = pltpu.get_barrier_semaphore()
    greeted = [partner, (lat, west), (lat, east), (north, lon), (south, lon), (north, west), (south, east)]
    greeted += [device((z + d) % 8, y, x, c) for d in range(1, 8)]
    greeted += [device(z, (y + d) % 4, x, c) for d in range(1, 4)]
    greeted += [device(z, y, (x + d) % 4, c) for d in range(1, 4)]
    for target in greeted:
        pl.semaphore_signal(barrier, inc=1, device_id=target, device_id_type=MESH)

    order = list(range(15)) + [15, 16, 17, 18]
    pairs_ = list(zip(list(tabs_h) + [wqkv_h, wo_h, wm_h, we_h], list(tabs) + [wqkv, wo, wm, we]))
    loads = [pltpu.make_async_copy(*pairs_[n], ws.at[n]) for n in order]
    for n in (0, 1, 2, 3, 4, 5, 12, 13, 14, 6, 7, 15, 16, 8, 9, 10, 17, 18, 11):
        loads[n].start()

    def remote(src, dst, send, recv, target):
        return pltpu.make_async_remote_copy(
            src_ref=src, dst_ref=dst, send_sem=send, recv_sem=recv, device_id=target, device_id_type=MESH
        )

    def segments(source, target, send, recv, s, across_lon, across_lat, names):
        places = (("B0", (lat, across_lon)), ("B1", (lat, across_lon)), ("C", (across_lat, lon)), ("D", (across_lat, across_lon)))
        return [
            remote(source.at[s, slice(*SEG[name])], target.at[s, slice(*SEG[name])], send.at[s, n], recv.at[s, n], to)
            for n, (name, to) in enumerate(places)
            if name in names
        ]

    def halo(s, names=REMOTE):
        return segments(snd, xb, hs, hr, s, west, north, names)

    def back(s, names=REMOTE):
        return segments(ret, zb, rs, rr, s, east, south, names)

    flags = remote(fl, fln, fs.at[0], fr.at[0], (north, lon))
    pair = remote(cw, pb, ps.at[0], pr.at[0], partner)

    def first():
        block = wg.at[y_lo, x, :, z, y_hi, c]
        return [
            remote(block, block, s2s.at[d - 1], s2r.at[d - 1], device(z, (y + d * (1 - c)) % 4, (x + d * c) % 4, c))
            for d in range(1, 4)
        ]

    def along_z(core, m):
        block = wg.at[:, x, m, z, :, 0] if core == 0 else wg.at[y_lo, :, m, z, y_hi, 1]
        return [
            remote(block, block, zs.at[m, d - 1], zr.at[m, d - 1], device((z + d) % 8, y, x, core)) for d in range(1, 8)
        ]

    def chunk(core, step, m):
        if core == 0:
            return wg.at[:, (x + step) % 4, m, :, :, 0]
        other = (y + step) % 4
        return wg.at[other % 2, :, m, :, other // 2, 1]

    def ring(core, step):
        return device(z, y, (x + step) % 4, core) if core == 0 else device(z, (y + step) % 4, x, core)

    def third(core, m):
        block = chunk(core, 0, slice(m, m + 1))
        return [remote(block, block, s3s.at[m, d - 1], s3r.at[m, d - 1], ring(core, d)) for d in range(1, 4)]

    def across(core, m, d):
        block = chunk(core, (4 - d) % 4, slice(m, m + 1))
        return remote(block, block, ds_.at[m, d], dr.at[m, d], partner)

    def on_core(action):
        @pl.when(c == 0)
        def _():
            action(0)

        @pl.when(c == 1)
        def _():
            action(1)

    pl.semaphore_wait(barrier, len(greeted))
    place = lax.broadcasted_iota(jnp.int32, (64, 128), 1) == lax.broadcasted_iota(jnp.int32, (64, 128), 0) + 64 * c
    place = jnp.where(place, 1.0, 0.0).astype(BF)
    cw[0:3] = dot(cqkv[...].reshape(192, 64), place).astype(BF).reshape(3, 64, 128)
    cw[3] = dot(cout[...], place).astype(BF)
    pair.start()
    spread = jnp.where(
        lax.broadcasted_iota(jnp.int32, (12, 128), 1) == lax.broadcasted_iota(jnp.int32, (12, 128), 0), 1.0, 0.0
    )
    flat = dot(jnp.broadcast_to(vr[...].astype(F32), (16, 12)).astype(BF), spread.astype(BF))
    corner = lax.broadcasted_iota(jnp.int32, (16, 128), 1) == lax.broadcasted_iota(jnp.int32, (16, 128), 0)
    fl[16:32] = flat.astype(BF)
    fl[0:16] = dot(jnp.where(corner, flat, 0.0).astype(BF), jnp.ones((128, 128), BF)).astype(BF)
    flags.start()

    pair.wait_recv()
    block = cw[...] + pb[...]
    wg[y_lo, x, :, z, y_hi, c] = jnp.where(c == 0, block[:, :32], block[:, 32:])
    for copy in first():
        copy.start()

    loads[0].wait()
    for s in range(2):
        tokens = dot(p1[...], xp[s * 144 : (s + 1) * 144].reshape(576, 512)).astype(BF)
        snd[s] = tokens
        for name in ("A0", "A1"):
            xb[s, slice(*SEG[name])] = tokens[slice(*SEG[name])]
        for copy in halo(s):
            copy.start()

    def poll_first():
        for copy in first():
            copy.wait_recv()

        def go(core):
            for m in range(2):
                for copy in along_z(core, m):
                    copy.start()

        on_core(go)

    def poll_z(m):
        def go(core):
            for copy in along_z(core, m):
                copy.wait_recv()
            later = along_z(core, m + 2) if m + 2 < 4 else []
            for copy in third(core, m) + [across(core, m, 0)] + later:
                copy.start()

        on_core(go)

    def poll_third(m):
        def go(core):
            arrivals = third(core, m)
            for d in (1, 3, 2):
                arrivals[d - 1].wait_recv()
                across(core, m, d).start()

        on_core(go)

    def arrived(m):
        def go(core):
            for d in range(4):
                across(core, m, d).wait_recv()

        on_core(go)

    poll_first()

    flags.wait_recv()
    for n in (1, 2, 3, 4, 5, 12, 13, 14):
        loads[n].wait()
    own, following = fl[...], fln[...]
    seam = jnp.where(lat == 15, NEG, 0.0)
    for w in range(2):
        down = dot(r1[w, :, 0:16], own[0:16]) + dot(r1[w, :, 16:32], following[0:16])
        flat = dot(own[16:32], rt[w, 0:128]) + dot(following[16:32], rt[w, 128:256])
        kcol[w * 144 : (w + 1) * 144] = down
        forbid = ((1.0 - flat[0:1]) * down[:, 0:1]) * NEG
        if w == 1:
            forbid = forbid + dm[...] * seam
        bias[0, w] = forbid
        bias[1, w] = forbid + lm[...] * NEG
    down = dot(rc[...], own[0:16])
    flat = dot(own[16:32], rct[...])
    cbias[...] = ((1.0 - flat[0:1]) * down[:, 0:1] + pads[0:1]) * NEG
    for parity in range(2):
        krow[parity] = dot(rk[parity], own[0:16])

    for n in (6, 7, 15, 16, 8, 9):
        loads[n].wait()

    def fine(s, w, after_qkv):
        for copy in halo(s, (("B0",), ("B1", "C", "D"))[w]):
            copy.wait_recv()
        low, high = UNIT[w]
        tokens = dot((p2a, p2b)[w][...], xb[s, low:high])
        xw[...] = tokens
        normed = normalised(tokens, 512).astype(BF)
        q[...] = (dot(normed, wqkv[:, 0:512]) * QSCALE).astype(BF)
        k[...] = dot(normed, wqkv[:, 512:1024]).astype(BF)
        v[...] = dot(normed, wqkv[:, 1024:1536]).astype(BF)
        after_qkv()
        for g in range(4):
            lanes = slice(g * 128, (g + 1) * 128)
            for group in range(2):
                rows = slice(group * 144, (group + 1) * 144)
                at[rows, lanes] = attention(q[rows, lanes], k[rows, lanes], v[rows, lanes], bias[group, w], False)
        keep = kcol[w * 144 : (w + 1) * 144, 0:1]
        skip = (xw[...] + dot(at[...], wo[...])).reshape(2, 144, 512) * keep[None]
        tokens = dot((p3a, p3b)[w][...], skip.reshape(288, 512).astype(BF)).astype(BF)
        ret[s, low:high] = tokens
        name = ("A0", "A1")[w]
        zb[s, slice(*SEG[name])] = tokens[slice(SEG[name][0] - low, SEG[name][1] - low)]
        for copy in back(s, (("B0",), ("B1", "C", "D"))[w]):
            copy.start()

    def nothing():
        return None

    fine(0, 0, nothing)
    fine(0, 1, nothing)
    fine(1, 1, nothing)
    poll_z(0)
    fine(1, 0, nothing)
    poll_z(1)
    poll_z(2)
    for n in (10, 17, 18, 11):
        loads[n].wait()

    for s in range(2):
        for copy in back(s):
            copy.wait_recv()
        planes = dot(p4[...], zb[s])
        skp[s] = planes.astype(BF)
        planes = planes.reshape(4, 160, 512)
        mean = jnp.sum(jnp.sum(planes, axis=0), axis=-1, keepdims=True) * (1.0 / 2048)
        centre = planes - mean[None]
        spread = jnp.sum(jnp.sum(centre * centre, axis=0), axis=-1, keepdims=True) * (1.0 / 2048)
        nbm[:, s * 160 : (s + 1) * 160] = (centre * lax.rsqrt(spread + EPSILON)[None]).astype(BF)

    poll_third(0)

    def merge(n, carry):
        lanes = pl.ds(pl.multiple_of(n * 256, 256), 256)
        total = dot(nbm[0], wm[0:512, lanes])
        for p in range(1, 4):
            total = total + dot(nbm[p], wm[512 * p : 512 * (p + 1), lanes])
        mg[:, lanes] = total.astype(BF)
        return carry

    lax.fori_loop(0, 4, merge, 0)
    n2[0] = normalised(mg[...].astype(F32), 1024).astype(BF)
    swap = remote(n2.at[0], n2.at[1], ns.at[0], nr.at[0], partner)
    swap.start()

    poll_third(1)
    poll_third(2)
    poll_z(3)
    arrived(0)

    def weights(matrix, n):
        low = (n % 2) * 2
        pieces = [wg[n // 2, low + j, matrix].reshape(1024, 128) for j in range(2)]
        return jnp.concatenate(pieces, axis=1)

    def queries(n, carry):
        lanes = pl.ds(pl.multiple_of(n * 256, 256), 256)
        q2[:, lanes] = (dot(n2[0], weights(0, n)) * QSCALE).astype(BF)
        return carry

    lax.fori_loop(0, 4, queries, 0)
    swap.wait_recv()

    def keys(matrix, block, carry):
        lanes = pl.ds(pl.multiple_of(block * 256, 256), 256)
        kv2[matrix, :, lanes] = dot(n2[...].reshape(640, 1024), weights(matrix + 1, block)).astype(BF)
        return carry

    for matrix in range(2):
        arrived(1 + matrix)
        lax.fori_loop(0, 4, functools.partial(keys, matrix), 0)

    def heads(half, carry):
        for g in range(4):
            lanes = pl.ds(pl.multiple_of(half * 512 + g * 128, 128), 128)
            for j in range(4):
                rows, far = slice(j * PADC, (j + 1) * PADC), slice(320 + j * PADC, 320 + (j + 1) * PADC)
                k4 = jnp.concatenate([kv2[0, rows, lanes], kv2[0, far, lanes]], axis=0)
                v4 = jnp.concatenate([kv2[1, rows, lanes], kv2[1, far, lanes]], axis=0)
                a2[rows, lanes] = attention(q2[rows, lanes], k4, v4, cbias[...], True)
        return carry

    lax.fori_loop(0, 2, heads, 0)
    poll_third(3)
    arrived(3)

    def project(n, carry):
        lanes = pl.ds(pl.multiple_of(n * 256, 256), 256)
        co[:, lanes] = (mg[:, lanes].astype(F32) + dot(a2[...], weights(3, n))).astype(BF)
        return carry

    lax.fori_loop(0, 4, project, 0)

    def expand(n, carry):
        plane, side = n // 2, n % 2
        grown = dot(co[...], we[:, pl.ds(pl.multiple_of(n * 256, 256), 256)])
        rows = pl.ds(pl.multiple_of(plane * 160, 160), 160)
        lanes = pl.ds(pl.multiple_of(side * 256, 256), 256)
        keep = krow[plane % 2][:, 0:1]
        for s in range(2):
            dc[s, rows, lanes] = ((skp[s, rows, lanes].astype(F32) + grown[s * 160 : (s + 1) * 160]) * keep).astype(BF)
        return carry

    lax.fori_loop(0, 8, expand, 0)
    for s in range(2):
        out[s * 144 : (s + 1) * 144] = dot(p5[...], dc[s]).astype(BF).reshape(144, 4, 512)

    pair.wait_send()
    flags.wait_send()
    swap.wait_send()
    for s in range(2):
        for copy in halo(s) + back(s):
            copy.wait_send()
    for copy in first():
        copy.wait_send()

    def go(core):
        for m in range(4):
            for copy in along_z(core, m) + third(core, m) + [across(core, m, d) for d in range(4)]:
                copy.wait_send()

    on_core(go)


def shards(fields, valid_rows, fine_qkv, fine_out, merge_weight, coarse_qkv, coarse_out, expand_weight):
    tabs = tables()
    xp = fields.transpose(0, 2, 3, 1, 4).reshape(288, 4, 512)
    operands = [xp, valid_rows.reshape(1, 12), coarse_qkv, coarse_out] + tabs
    operands += [fine_qkv, fine_out, merge_weight, expand_weight]
    vmem = pl.BlockSpec(memory_space=pltpu.VMEM)
    anywhere = pl.BlockSpec(memory_space=pl.ANY)
    dma = pltpu.SemaphoreType.DMA
    scratch = [pltpu.VMEM(a.shape, a.dtype) for a in tabs]
    scratch += [pltpu.VMEM(a.shape, BF) for a in (fine_qkv, fine_out, merge_weight, expand_weight)]
    scratch += [pltpu.VMEM((2, TOKENS, 512), BF)] * 4
    scratch += [pltpu.VMEM((32, 128), BF)] * 2 + [pltpu.VMEM((4, 64, 128), BF)] * 2
    scratch += [pltpu.VMEM((2, 4, 4, 8, 2, 2, 32, 128), BF)]
    scratch += [pltpu.VMEM((288, 512), F32)] + [pltpu.VMEM((288, 512), BF)] * 4
    scratch += [pltpu.VMEM((288, 128), F32), pltpu.VMEM((2, 2, 144, 144), F32)]
    scratch += [pltpu.VMEM((PADC, 2 * PADC), F32), pltpu.VMEM((2, 2 * PADC, 128), F32)]
    scratch += [pltpu.VMEM((2, 640, 512), BF), pltpu.VMEM((4, 320, 512), BF)]
    scratch += [pltpu.VMEM((320, 1024), BF), pltpu.VMEM((2, 320, 1024), BF)]
    scratch += [pltpu.VMEM((320, 1024), BF), pltpu.VMEM((2, 640, 1024), BF)]
    scratch += [pltpu.VMEM((320, 1024), BF)] * 2 + [pltpu.VMEM((2, 640, 512), BF)]
    for shape in ((2, 4), (2, 4), (1,), (1,), (4, 7), (3,), (4, 3), (4, 4), (1,)):
        scratch += [dma(shape), dma(shape)]
    scratch += [dma((19,))]
    result = pl.pallas_call(
        kernel,
        out_shape=jax.ShapeDtypeStruct((288, 4, 512), BF),
        in_specs=[vmem] * 4 + [anywhere] * 19,
        out_specs=vmem,
        scratch_shapes=scratch,
        compiler_params=pltpu.CompilerParams(collective_id=0, has_side_effects=True, vmem_limit_bytes=60 * 2**20),
    )(*operands)
    return result.reshape(2, 12, 12, 4, 512).transpose(0, 3, 1, 2, 4)


def solution(mesh):
    return jax.shard_map(
        shards,
        mesh=mesh,
        in_specs=(
            P(None, None, "lat", "lon", None),
            P("lat"),
            P(),
            P(),
            P(),
            P(None, "lat", "lon"),
            P("lat", "lon"),
            P(),
        ),
        out_specs=P(None, None, "lat", "lon", None),
        check_vma=False,
    )
```

```python
import functools
import math

import jax
import jax.numpy as jnp
import numpy as np
from jax import lax
from jax.experimental import pallas as pl
from jax.experimental.pallas import tpu as pltpu
from jax.sharding import PartitionSpec as P

BF = jnp.bfloat16
F32 = jnp.float32
MESH = pl.DeviceIdType.MESH
EPSILON = 1e-05
NEG = -1e30
QSCALE = 32 ** (-0.5) * math.log2(math.e)

SEG = dict(A0=(0, 144), B0=(144, 288), A1=(288, 368), B1=(368, 448), C=(448, 528), D=(528, 608))
TOKENS = 608
REMOTE = ("B0", "B1", "C", "D")
UNIT = ((0, 288), (288, 608))
LEVELS = ((1, 2), (3, 0))
PADC = 80


def segment_row(level_index, r, c):
    east = c >= 6
    if 3 <= r < 9:
        name, rows, row = "A0" if east else "B0", 6, r - 3
    elif r >= 9:
        name, rows, row = "A1" if east else "B1", 3, r - 9
    else:
        name, rows, row = "C" if east else "D", 3, r
    return SEG[name][0] + (level_index * rows + row) * 6 + c % 6


def window_row(level_index, r, c):
    row = r - 3 if 3 <= r < 9 else (r - 9 if r >= 9 else r + 3)
    column = c - 6 if c >= 6 else c + 6
    return level_index * 72 + row * 12 + column


def coarse_row(level, row, column):
    return (level // 2) * PADC + (level % 2) * 36 + row * 6 + column


def tables():
    p1 = np.zeros((TOKENS, 576), np.float32)
    p2 = np.zeros((288, TOKENS), np.float32)
    p4 = np.zeros((4 * 2 * PADC, TOKENS), np.float32)
    p5 = np.zeros((576, 4 * 2 * PADC), np.float32)
    for r in range(12):
        for c in range(12):
            plane = (r % 2) + 2 * (c % 2)
            for index in range(4):
                level = LEVELS[index // 2][index % 2]
                seg = segment_row(index, r, c)
                place = (r * 12 + c) * 4 + level
                low = plane * 2 * PADC + coarse_row(level, r // 2, c // 2)
                p1[seg, place] = 1
                p2[window_row(index, r, c), seg] = 1
                p4[low, seg] = 1
                p5[place, low] = 1
    rows = np.zeros((2, 144, 32), np.float32)
    differ = np.zeros((144, 144), np.float32)
    level = np.zeros((144, 144), np.float32)
    for t in range(144):
        r6 = (t % 72) // 12
        rows[0, t, 3 + r6] = 1
        rows[1, t, 9 + r6 if r6 < 3 else 16 + r6 - 3] = 1
        for u in range(144):
            differ[t, u] = (r6 < 3) != ((u % 72) // 12 < 3)
            level[t, u] = (t // 72) != (u // 72)
    rows_t = np.zeros((2, 256, 144), np.float32)
    rows_t[:, 0:12] = rows.transpose(0, 2, 1)[:, 0:12]
    rows_t[:, 128:131] = rows.transpose(0, 2, 1)[:, 16:19]
    coarse = np.zeros((PADC, 16), np.float32)
    keep = np.zeros((2, 2 * PADC, 16), np.float32)
    for t in range(72):
        row = (t % 36) // 6
        coarse[t, 2 * row] = 1
        for group in range(2):
            for parity in range(2):
                keep[parity, group * PADC + t, 2 * row + parity] = 1
    coarse_t = np.zeros((128, 2 * PADC), np.float32)
    coarse_t[0:16, :PADC] = coarse.T
    coarse_t[0:16, PADC:] = coarse.T
    pads = np.zeros((8, 2 * PADC), np.float32)
    pads[:, np.arange(2 * PADC) % PADC >= 72] = 1
    ways = [p2[:, low:high] for low, high in UNIT]
    half = [p1, rows, rows_t, coarse, coarse_t, keep] + ways + [w.T.copy() for w in ways] + [p4, p5]
    return [jnp.asarray(a, BF) for a in half] + [jnp.asarray(a, F32) for a in (level, differ, pads)]


def dot(a, b):
    return jnp.dot(a, b, preferred_element_type=F32)


def dot_nt(a, b):
    return lax.dot_general(a, b, (((1,), (1,)), ((), ())), preferred_element_type=F32)


def normalised(x, width):
    mean = jnp.sum(x, axis=-1, keepdims=True) * (1.0 / width)
    centre = x - mean
    spread = jnp.sum(centre * centre, axis=-1, keepdims=True) * (1.0 / width)
    return centre * lax.rsqrt(spread + EPSILON)


def head_masks():
    head = lax.broadcasted_iota(jnp.int32, (16, 128), 1) // 32
    return [jnp.where(head == h, 1.0, 0.0).astype(BF)[0:1] for h in range(4)]


def weighed(expo, v4, mask):
    return dot(expo, jnp.concatenate([v4 * mask, jnp.broadcast_to(mask, v4.shape)], axis=1))


def attention(q4, k4, v4, bias, together):
    masks = head_masks()
    count = q4.shape[0]
    if together:
        scores = dot_nt(jnp.concatenate([q4 * m for m in masks], axis=0), k4)
    total = 0.0
    for h, mask in enumerate(masks):
        mine = (scores[h * count : (h + 1) * count] if together else dot_nt(q4 * mask, k4)) + bias
        expo = jnp.exp2(mine - jnp.max(mine, axis=-1, keepdims=True)).astype(BF)
        total = total + weighed(expo, v4, mask)
    return (total[:, :128] / total[:, 128:]).astype(BF)


def kernel(
    xp, vr, cqkv, cout, *rest
):
    tabs_h, (wqkv_h, wo_h, wm_h, we_h), out, rest = rest[:15], rest[15:19], rest[19], rest[20:]
    tabs, (wqkv, wo, wm, we), rest = rest[:15], rest[15:19], rest[19:]
    p1, r1, rt, rc, rct, rk, p2a, p2b, p3a, p3b, p4, p5, lm, dm, pads = tabs
    snd, xb, ret, zb, fl, fln, cw, pb, wg, xw, q, k, v, at, kcol, bias, cbias, krow, *rest = rest
    skp, nbm, mg, n2, q2, kv2, a2, co, dc, *rest = rest
    hs, hr, rs, rr, fs, fr, ps, pr, zs, zr, s2s, s2r, s3s, s3r, ds_, dr, ns, nr, ws = rest
    lat = lax.axis_index("lat")
    lon = lax.axis_index("lon")
    z, y_hi = lat // 2, lat % 2
    y_lo, x, c = lon // 8, (lon // 2) % 4, lon % 2
    y = y_hi * 2 + y_lo

    def device(z_, y_, x_, c_):
        return (z_ * 2 + y_ // 2, (y_ % 2) * 8 + x_ * 2 + c_)

    north, south = (lat + 15) % 16, (lat + 1) % 16
    west, east = (lon + 15) % 16, (lon + 1) % 16
    partner = device(z, y, x, 1 - c)

    barrier = pltpu.get_barrier_semaphore()
    greeted = [partner, (lat, west), (lat, east), (north, lon), (south, lon), (north, west), (south, east)]
    greeted += [device((z + d) % 8, y, x, c) for d in range(1, 8)]
    greeted += [device(z, (y + d) % 4, x, c) for d in range(1, 4)]
    greeted += [device(z, y, (x + d) % 4, c) for d in range(1, 4)]
    for target in greeted:
        pl.semaphore_signal(barrier, inc=1, device_id=target, device_id_type=MESH)

    order = list(range(15)) + [15, 16, 17, 18]
    pairs_ = list(zip(list(tabs_h) + [wqkv_h, wo_h, wm_h, we_h], list(tabs) + [wqkv, wo, wm, we]))
    loads = [pltpu.make_async_copy(*pairs_[n], ws.at[n]) for n in order]
    for n in (0, 1, 2, 3, 4, 5, 12, 13, 14, 6, 7, 15, 16, 8, 9, 10, 17, 18, 11):
        loads[n].start()

    def remote(src, dst, send, recv, target):
        return pltpu.make_async_remote_copy(
            src_ref=src, dst_ref=dst, send_sem=send, recv_sem=recv, device_id=target, device_id_type=MESH
        )

    def segments(source, target, send, recv, s, across_lon, across_lat, names):
        places = (("B0", (lat, across_lon)), ("B1", (lat, across_lon)), ("C", (across_lat, lon)), ("D", (across_lat, across_lon)))
        return [
            remote(source.at[s, slice(*SEG[name])], target.at[s, slice(*SEG[name])], send.at[s, n], recv.at[s, n], to)
            for n, (name, to) in enumerate(places)
            if name in names
        ]

    def halo(s, names=REMOTE):
        return segments(snd, xb, hs, hr, s, west, north, names)

    def back(s, names=REMOTE):
        return segments(ret, zb, rs, rr, s, east, south, names)

    flags = remote(fl, fln, fs.at[0], fr.at[0], (north, lon))
    pair = remote(cw, pb, ps.at[0], pr.at[0], partner)

    def first():
        block = wg.at[y_lo, x, :, z, y_hi, c]
        return [
            remote(block, block, s2s.at[d - 1], s2r.at[d - 1], device(z, (y + d * (1 - c)) % 4, (x + d * c) % 4, c))
            for d in range(1, 4)
        ]

    def along_z(core, m):
        block = wg.at[:, x, m, z, :, 0] if core == 0 else wg.at[y_lo, :, m, z, y_hi, 1]
        return [
            remote(block, block, zs.at[m, d - 1], zr.at[m, d - 1], device((z + d) % 8, y, x, core)) for d in range(1, 8)
        ]

    def chunk(core, step, m):
        if core == 0:
            return wg.at[:, (x + step) % 4, m, :, :, 0]
        other = (y + step) % 4
        return wg.at[other % 2, :, m, :, other // 2, 1]

    def ring(core, step):
        return device(z, y, (x + step) % 4, core) if core == 0 else device(z, (y + step) % 4, x, core)

    def third(core, m):
        block = chunk(core, 0, slice(m, m + 1))
        return [remote(block, block, s3s.at[m, d - 1], s3r.at[m, d - 1], ring(core, d)) for d in range(1, 4)]

    def across(core, m, d):
        block = chunk(core, (4 - d) % 4, slice(m, m + 1))
        return remote(block, block, ds_.at[m, d], dr.at[m, d], partner)

    def on_core(action):
        @pl.when(c == 0)
        def _():
            action(0)

        @pl.when(c == 1)
        def _():
            action(1)

    pl.semaphore_wait(barrier, len(greeted))
    place = lax.broadcasted_iota(jnp.int32, (64, 128), 1) == lax.broadcasted_iota(jnp.int32, (64, 128), 0) + 64 * c
    place = jnp.where(place, 1.0, 0.0).astype(BF)
    cw[0:3] = dot(cqkv[...].reshape(192, 64), place).astype(BF).reshape(3, 64, 128)
    cw[3] = dot(cout[...], place).astype(BF)
    pair.start()
    spread = jnp.where(
        lax.broadcasted_iota(jnp.int32, (12, 128), 1) == lax.broadcasted_iota(jnp.int32, (12, 128), 0), 1.0, 0.0
    )
    flat = dot(jnp.broadcast_to(vr[...].astype(F32), (16, 12)).astype(BF), spread.astype(BF))
    corner = lax.broadcasted_iota(jnp.int32, (16, 128), 1) == lax.broadcasted_iota(jnp.int32, (16, 128), 0)
    fl[16:32] = flat.astype(BF)
    fl[0:16] = dot(jnp.where(corner, flat, 0.0).astype(BF), jnp.ones((128, 128), BF)).astype(BF)
    flags.start()

    pair.wait_recv()
    block = cw[...] + pb[...]
    wg[y_lo, x, :, z, y_hi, c] = jnp.where(c == 0, block[:, :32], block[:, 32:])
    for copy in first():
        copy.start()

    loads[0].wait()
    for s in range(2):
        tokens = dot(p1[...], xp[s * 144 : (s + 1) * 144].reshape(576, 512)).astype(BF)
        snd[s] = tokens
        for name in ("A0", "A1"):
            xb[s, slice(*SEG[name])] = tokens[slice(*SEG[name])]
        for copy in halo(s):
            copy.start()

    def poll_first():
        for copy in first():
            copy.wait_recv()

        def go(core):
            for m in range(2):
                for copy in along_z(core, m):
                    copy.start()

        on_core(go)

    def poll_z(m):
        def go(core):
            for copy in along_z(core, m):
                copy.wait_recv()
            later = along_z(core, m + 2) if m + 2 < 4 else []
            for copy in third(core, m) + [across(core, m, 0)] + later:
                copy.start()

        on_core(go)

    def poll_third(m):
        def go(core):
            arrivals = third(core, m)
            for d in (1, 3, 2):
                arrivals[d - 1].wait_recv()
                across(core, m, d).start()

        on_core(go)

    def arrived(m):
        def go(core):
            for d in range(4):
                across(core, m, d).wait_recv()

        on_core(go)

    poll_first()

    flags.wait_recv()
    for n in (1, 2, 3, 4, 5, 12, 13, 14):
        loads[n].wait()
    own, following = fl[...], fln[...]
    seam = jnp.where(lat == 15, NEG, 0.0)
    for w in range(2):
        down = dot(r1[w, :, 0:16], own[0:16]) + dot(r1[w, :, 16:32], following[0:16])
        flat = dot(own[16:32], rt[w, 0:128]) + dot(following[16:32], rt[w, 128:256])
        kcol[w * 144 : (w + 1) * 144] = down
        forbid = ((1.0 - flat[0:1]) * down[:, 0:1]) * NEG
        if w == 1:
            forbid = forbid + dm[...] * seam
        bias[0, w] = forbid
        bias[1, w] = forbid + lm[...] * NEG
    down = dot(rc[...], own[0:16])
    flat = dot(own[16:32], rct[...])
    cbias[...] = ((1.0 - flat[0:1]) * down[:, 0:1] + pads[0:1]) * NEG
    for parity in range(2):
        krow[parity] = dot(rk[parity], own[0:16])

    for n in (6, 7, 15, 16, 8, 9):
        loads[n].wait()

    def fine(s, w, after_qkv):
        for copy in halo(s, (("B0",), ("B1", "C", "D"))[w]):
            copy.wait_recv()
        low, high = UNIT[w]
        tokens = dot((p2a, p2b)[w][...], xb[s, low:high])
        xw[...] = tokens
        normed = normalised(tokens, 512).astype(BF)
        q[...] = (dot(normed, wqkv[:, 0:512]) * QSCALE).astype(BF)
        k[...] = dot(normed, wqkv[:, 512:1024]).astype(BF)
        v[...] = dot(normed, wqkv[:, 1024:1536]).astype(BF)
        after_qkv()
        for g in range(4):
            lanes = slice(g * 128, (g + 1) * 128)
            for group in range(2):
                rows = slice(group * 144, (group + 1) * 144)
                at[rows, lanes] = attention(q[rows, lanes], k[rows, lanes], v[rows, lanes], bias[group, w], False)
        keep = kcol[w * 144 : (w + 1) * 144, 0:1]
        skip = (xw[...] + dot(at[...], wo[...])).reshape(2, 144, 512) * keep[None]
        tokens = dot((p3a, p3b)[w][...], skip.reshape(288, 512).astype(BF)).astype(BF)
        ret[s, low:high] = tokens
        name = ("A0", "A1")[w]
        zb[s, slice(*SEG[name])] = tokens[slice(SEG[name][0] - low, SEG[name][1] - low)]
        for copy in back(s, (("B0",), ("B1", "C", "D"))[w]):
            copy.start()

    def nothing():
        return None

    fine(0, 0, nothing)
    fine(0, 1, nothing)
    fine(1, 1, nothing)
    poll_z(0)
    fine(1, 0, nothing)
    poll_z(1)
    poll_z(2)
    for n in (10, 17, 18, 11):
        loads[n].wait()

    for s in range(2):
        for copy in back(s):
            copy.wait_recv()
        planes = dot(p4[...], zb[s])
        skp[s] = planes.astype(BF)
        planes = planes.reshape(4, 160, 512)
        mean = jnp.sum(jnp.sum(planes, axis=0), axis=-1, keepdims=True) * (1.0 / 2048)
        centre = planes - mean[None]
        spread = jnp.sum(jnp.sum(centre * centre, axis=0), axis=-1, keepdims=True) * (1.0 / 2048)
        nbm[:, s * 160 : (s + 1) * 160] = (centre * lax.rsqrt(spread + EPSILON)[None]).astype(BF)

    def merge(n, carry):
        lanes = pl.ds(pl.multiple_of(n * 256, 256), 256)
        total = dot(nbm[0], wm[0:512, lanes])
        for p in range(1, 4):
            total = total + dot(nbm[p], wm[512 * p : 512 * (p + 1), lanes])
        mg[:, lanes] = total.astype(BF)
        return carry

    lax.fori_loop(0, 4, merge, 0, unroll=2)
    n2[0] = normalised(mg[...].astype(F32), 1024).astype(BF)
    swap = remote(n2.at[0], n2.at[1], ns.at[0], nr.at[0], partner)
    swap.start()

    poll_third(0)
    poll_third(1)
    arrived(0)

    def weights(matrix, n):
        low = (n % 2) * 2
        pieces = [wg[n // 2, low + j, matrix].reshape(1024, 128) for j in range(2)]
        return jnp.concatenate(pieces, axis=1)

    def queries(n, carry):
        lanes = pl.ds(pl.multiple_of(n * 256, 256), 256)
        q2[:, lanes] = (dot(n2[0], weights(0, n)) * QSCALE).astype(BF)
        return carry

    lax.fori_loop(0, 4, queries, 0, unroll=2)
    poll_third(2)
    poll_z(3)
    swap.wait_recv()

    def keys(matrix, block, carry):
        lanes = pl.ds(pl.multiple_of(block * 256, 256), 256)
        kv2[matrix, :, lanes] = dot(n2[...].reshape(640, 1024), weights(matrix + 1, block)).astype(BF)
        return carry

    for matrix in range(2):
        arrived(1 + matrix)
        lax.fori_loop(0, 4, functools.partial(keys, matrix), 0, unroll=2)

    def heads(half, carry):
        for g in range(4):
            lanes = pl.ds(pl.multiple_of(half * 512 + g * 128, 128), 128)
            for j in range(4):
                rows, far = slice(j * PADC, (j + 1) * PADC), slice(320 + j * PADC, 320 + (j + 1) * PADC)
                k4 = jnp.concatenate([kv2[0, rows, lanes], kv2[0, far, lanes]], axis=0)
                v4 = jnp.concatenate([kv2[1, rows, lanes], kv2[1, far, lanes]], axis=0)
                a2[rows, lanes] = attention(q2[rows, lanes], k4, v4, cbias[...], True)
        return carry

    lax.fori_loop(0, 2, heads, 0)
    poll_third(3)
    arrived(3)

    def project(n, carry):
        lanes = pl.ds(pl.multiple_of(n * 256, 256), 256)
        co[:, lanes] = (mg[:, lanes].astype(F32) + dot(a2[...], weights(3, n))).astype(BF)
        return carry

    lax.fori_loop(0, 4, project, 0, unroll=4)

    def expand(n, carry):
        plane, side = n // 2, n % 2
        grown = dot(co[...], we[:, pl.ds(pl.multiple_of(n * 256, 256), 256)])
        rows = pl.ds(pl.multiple_of(plane * 160, 160), 160)
        lanes = pl.ds(pl.multiple_of(side * 256, 256), 256)
        keep = krow[plane % 2][:, 0:1]
        for s in range(2):
            dc[s, rows, lanes] = ((skp[s, rows, lanes].astype(F32) + grown[s * 160 : (s + 1) * 160]) * keep).astype(BF)
        return carry

    lax.fori_loop(0, 8, expand, 0, unroll=4)
    for s in range(2):
        out[s * 144 : (s + 1) * 144] = dot(p5[...], dc[s]).astype(BF).reshape(144, 4, 512)

    pair.wait_send()
    flags.wait_send()
    swap.wait_send()
    for s in range(2):
        for copy in halo(s) + back(s):
            copy.wait_send()
    for copy in first():
        copy.wait_send()

    def go(core):
        for m in range(4):
            for copy in along_z(core, m) + third(core, m) + [across(core, m, d) for d in range(4)]:
                copy.wait_send()

    on_core(go)


def shards(fields, valid_rows, fine_qkv, fine_out, merge_weight, coarse_qkv, coarse_out, expand_weight):
    tabs = tables()
    xp = fields.transpose(0, 2, 3, 1, 4).reshape(288, 4, 512)
    operands = [xp, valid_rows.reshape(1, 12), coarse_qkv, coarse_out] + tabs
    operands += [fine_qkv, fine_out, merge_weight, expand_weight]
    vmem = pl.BlockSpec(memory_space=pltpu.VMEM)
    anywhere = pl.BlockSpec(memory_space=pl.ANY)
    dma = pltpu.SemaphoreType.DMA
    scratch = [pltpu.VMEM(a.shape, a.dtype) for a in tabs]
    scratch += [pltpu.VMEM(a.shape, BF) for a in (fine_qkv, fine_out, merge_weight, expand_weight)]
    scratch += [pltpu.VMEM((2, TOKENS, 512), BF)] * 4
    scratch += [pltpu.VMEM((32, 128), BF)] * 2 + [pltpu.VMEM((4, 64, 128), BF)] * 2
    scratch += [pltpu.VMEM((2, 4, 4, 8, 2, 2, 32, 128), BF)]
    scratch += [pltpu.VMEM((288, 512), F32)] + [pltpu.VMEM((288, 512), BF)] * 4
    scratch += [pltpu.VMEM((288, 128), F32), pltpu.VMEM((2, 2, 144, 144), F32)]
    scratch += [pltpu.VMEM((PADC, 2 * PADC), F32), pltpu.VMEM((2, 2 * PADC, 128), F32)]
    scratch += [pltpu.VMEM((2, 640, 512), BF), pltpu.VMEM((4, 320, 512), BF)]
    scratch += [pltpu.VMEM((320, 1024), BF), pltpu.VMEM((2, 320, 1024), BF)]
    scratch += [pltpu.VMEM((320, 1024), BF), pltpu.VMEM((2, 640, 1024), BF)]
    scratch += [pltpu.VMEM((320, 1024), BF)] * 2 + [pltpu.VMEM((2, 640, 512), BF)]
    for shape in ((2, 4), (2, 4), (1,), (1,), (4, 7), (3,), (4, 3), (4, 4), (1,)):
        scratch += [dma(shape), dma(shape)]
    scratch += [dma((19,))]
    result = pl.pallas_call(
        kernel,
        out_shape=jax.ShapeDtypeStruct((288, 4, 512), BF),
        in_specs=[vmem] * 4 + [anywhere] * 19,
        out_specs=vmem,
        scratch_shapes=scratch,
        compiler_params=pltpu.CompilerParams(collective_id=0, has_side_effects=True, vmem_limit_bytes=60 * 2**20),
    )(*operands)
    return result.reshape(2, 12, 12, 4, 512).transpose(0, 3, 1, 2, 4)


def solution(mesh):
    return jax.shard_map(
        shards,
        mesh=mesh,
        in_specs=(
            P(None, None, "lat", "lon", None),
            P("lat"),
            P(),
            P(),
            P(),
            P(None, "lat", "lon"),
            P("lat", "lon"),
            P(),
        ),
        out_specs=P(None, None, "lat", "lon", None),
        check_vma=False,
    )
```
